128 devices in a mesh: rows: 8 (over y, core), keys: 16 (over z, x).
Axes of the slice: x: 4, y: 4, z: 4, core: 2. Of those that a mesh axis runs over, the one named last changes fastest.
Arguments:
- pair_rep: bfloat16 [512, 512, 128], P('rows', 'keys'), may hold values from -6 to 6
- token_mask: int32 [512], replicated, may hold values from 0 to 1, as said below
- norm_gain: float32 [2, 128], replicated, may hold values from 0.5 to 1.5
- norm_shift: float32 [2, 128], replicated, may hold values from -0.5 to 0.5
- w_proj: bfloat16 [2, 128, 512], replicated, may hold values from -1 to 1
- w_bias: bfloat16 [2, 128, 4], replicated, may hold values from -0.25 to 0.25
- gate_bias: float32 [2, 128], replicated, may hold values from -1.5 to 1.5
- w_out: bfloat16 [2, 128, 128], replicated, may hold values from -0.5 to 0.5
Outputs:
- new_pair: bfloat16 [512, 512, 128], P('rows', 'keys')
The draws below stay inside these ranges and needn't reach their ends.
Inputs may be any that keep to these rules, and one draw needn't show every extreme that they name: token_mask is 1 on a leading run of at least 256 tokens and 0 on the rest, with at least one 0.
All inputs are finite; a program needn't handle non-finite values.
Results may differ from the reference program's by a relative error of at most 0.02.
Values may be sent and summed in bfloat16 or wider, within the bound.
A program may use at most 128 MiB of HBM per device.

```python
import jax
import jax.numpy as jnp
from jax import lax

C = 128
H = 4
D = 32
HD = 128
TOKENS = 512


def draw_token_mask(key, part):
    key = jax.random.fold_in(key, 5)
    valid = jax.random.randint(key, (), TOKENS // 2, TOKENS)
    return (jnp.arange(TOKENS) < valid).astype(jnp.int32)


def draw_w_bias(key, part):
    key = jax.random.fold_in(key, 11)
    values = jnp.clip(jax.random.normal(key, (2, C, H), jnp.float32) * (2.0 / C) ** 0.5, -0.25, 0.25)
    return values.astype(jnp.bfloat16)


def shard_levels(key, shape, shards, smallest, top_value):
    gain = 1.0
    for position, shards_of in shards:
        heights = jax.random.uniform(jax.random.fold_in(jax.random.fold_in(key, 6), position), (shards_of,), jnp.float32, smallest / len(shards), top_value / len(shards))
        gain = gain * jnp.repeat(jnp.exp(heights), shape[position] // shards_of).reshape((-1,) + (1,) * (len(shape) - 1 - position))
    return gain


def centred(rng, extent, scale, most, split=(), dtype=jnp.bfloat16):
    loudness = shard_levels(rng, extent, split, -0.22, 0.18) if split else 1.0
    result = jax.random.normal(rng, extent, jnp.float32) * scale * loudness
    return jnp.minimum(jnp.maximum(result, -most), most).astype(dtype)


def setup_inputs(seed: int = 0) -> dict:
    seeds = jax.random.split(jax.random.key(seed), 9)
    pair_rep = centred(seeds[0], (TOKENS, TOKENS, C), 1.0, 6.0, ((0, 8), (1, 16)))
    token_mask = draw_token_mask(jax.random.fold_in(seeds[8], 71), 0)
    norm_gain = jnp.clip(1.0 + 0.1 * jax.random.normal(seeds[2], (2, C), jnp.float32), 0.5, 1.5)
    norm_shift = jnp.clip(jax.random.uniform(seeds[3], (2, C), jnp.float32, -0.5, 0.5), -0.5, 0.5)
    w_proj = centred(seeds[4], (2, C, 4 * HD), (C // 4) ** -0.5, 1.0)
    w_bias = draw_w_bias(jax.random.fold_in(seeds[8], 71), 0)
    gate_bias = jnp.clip(jax.random.uniform(seeds[6], (2, HD), jnp.float32, -1.5, 1.5), -1.5, 1.5)
    w_out = centred(seeds[7], (2, HD, C), HD ** -0.5, 0.5)
    return dict(pair_rep=pair_rep, token_mask=token_mask, norm_gain=norm_gain, norm_shift=norm_shift, w_proj=w_proj, w_bias=w_bias, gate_bias=gate_bias, w_out=w_out)


def stored(values):
    return lax.optimization_barrier(values.astype(jnp.bfloat16)).astype(jnp.float32)

def layer_norm(values, norm_gain, norm_shift):
    center = lax.optimization_barrier(jnp.mean(values, axis=-1, keepdims=True))
    spread = lax.optimization_barrier(jnp.mean((values - center) ** 2, axis=-1, keepdims=True))
    return (values - center) * lax.rsqrt(spread + 1e-05) * norm_gain + norm_shift

def triangle_pass(pair_array, key_bias, which, norm_gain, norm_shift, w_proj, w_bias, gate_bias, w_out):
    normed = layer_norm(pair_array.astype(jnp.float32), norm_gain[which], norm_shift[which]).astype(jnp.bfloat16)
    flat_rows = normed.reshape(TOKENS * TOKENS, C)
    projected = jnp.dot(flat_rows, w_proj[which], preferred_element_type=jnp.float32)
    queries = stored(projected[:, :HD] * D ** (-0.5)).reshape(TOKENS, TOKENS, H, D)
    key_part = stored(projected[:, HD:2 * HD]).reshape(TOKENS, TOKENS, H, D)
    value_part = stored(projected[:, 2 * HD:3 * HD]).reshape(TOKENS, TOKENS, H, D)
    gating = jax.nn.sigmoid(projected[:, 3 * HD:] + gate_bias[which])
    pair_bias = stored(jnp.dot(flat_rows, w_bias[which], preferred_element_type=jnp.float32))
    score_bias = pair_bias.reshape(TOKENS, TOKENS, H).transpose(0, 2, 1) + key_bias[None, None, :]
    row_block = 16

    def attend_block(operands):
        query_rows, key_rows, value_rows = operands
        scores = jnp.einsum('ijhd,ikhd->ijhk', query_rows, key_rows) + score_bias[None]
        peak = lax.optimization_barrier(jnp.max(scores, axis=-1, keepdims=True))
        expo = jnp.exp(scores - peak)
        denom = lax.optimization_barrier(jnp.sum(expo, axis=-1))
        weights = stored(expo)
        summed = jnp.einsum('ijhk,ikhd->ijhd', weights, value_rows)
        return summed / denom[..., None]
    shape_blocks = (TOKENS // row_block, row_block, TOKENS, H, D)
    attended = lax.map(attend_block, (queries.reshape(shape_blocks), key_part.reshape(shape_blocks), value_part.reshape(shape_blocks)))
    gated = (attended.reshape(TOKENS * TOKENS, HD) * gating).astype(jnp.bfloat16)
    return jnp.dot(gated, w_out[which], preferred_element_type=jnp.float32).reshape(TOKENS, TOKENS, C)

def reference(pair_rep, token_mask, norm_gain, norm_shift, w_proj, w_bias, gate_bias, w_out):
    mask_float = token_mask.astype(jnp.float32)
    key_bias = (mask_float - 1.0) * 1000000000.0
    pair_mask = (mask_float[:, None] * mask_float[None, :])[..., None]
    weights_all = (norm_gain, norm_shift, w_proj, w_bias, gate_bias, w_out)
    start_branch = triangle_pass(pair_rep, key_bias, 0, *weights_all)
    after_start = (pair_rep.astype(jnp.float32) + pair_mask * start_branch).astype(jnp.bfloat16)
    end_branch = triangle_pass(after_start.transpose(1, 0, 2), key_bias, 1, *weights_all)
    end_update = (pair_mask * end_branch.transpose(1, 0, 2)).astype(jnp.bfloat16)
    return (after_start.astype(jnp.float32) + end_update.astype(jnp.float32)).astype(jnp.bfloat16)
```

```python
import functools

import jax
import jax.numpy as jnp
from jax import lax
from jax.experimental import pallas as pl
from jax.experimental.pallas import tpu as pltpu
from jax.sharding import PartitionSpec as P

MESH = pl.DeviceIdType.MESH
LOG2E = 1.4426950408889634
F32 = jnp.float32
BF16 = jnp.bfloat16
KEYS = 32
HEADS = 4
HEAD = 32
LANES = 128
CHUNK = 256


def layer_norm(values, gain, shift):
    center = jnp.mean(values, axis=-1, keepdims=True)
    moved = values - center
    spread = jnp.mean(moved * moved, axis=-1, keepdims=True)
    return moved * lax.rsqrt(spread + 1e-05) * gain + shift


def head_max(m, lane):
    for step in (16, 8, 4, 2, 1):
        below = pltpu.roll(m, step, 1)
        above = pltpu.roll(m, LANES - step, 1)
        m = jnp.maximum(m, jnp.where((lane & step) != 0, below, above))
    return m


def kernel(
    tokens, row_n, key_n,
    x_ref, kb_ref, mk_ref, gain_ref, shift_ref, wp_ref, wb_ref, gb_ref, wo_ref,
    out_ref,
    x1, x2, as1, np2, t2, sb, fin, tile_f, bias_a, bias_b, bias_s, q_s, k_s, v_s, g_s, s_s,
    a1_send, a1_recv, a2_send, a2_recv, b2_send, b2_recv, c2_send, c2_recv,
    ga_send, ga_recv, gb_send, gb_recv,
):
    rows_t, cols_t = tokens // row_n, tokens // key_n
    per = tokens // (row_n * key_n)
    groups = tokens // KEYS
    y_n = row_n // 2
    z_n = x_n = int(round(key_n**0.5))
    y_h = y_n // 2
    r, c = lax.axis_index("rows"), lax.axis_index("keys")
    y, core = r // 2, r % 2
    z, xx = c // x_n, c % x_n
    lane = lax.broadcasted_iota(jnp.int32, (1, LANES), 1)

    barrier = pltpu.get_barrier_semaphore()

    def greet_keys(o, carry):
        pl.semaphore_signal(barrier, inc=1, device_id=(r, lax.rem(c + o, key_n)), device_id_type=MESH)
        return carry

    def greet_rows(o, carry):
        pl.semaphore_signal(barrier, inc=1, device_id=(lax.rem(r + o, row_n), c), device_id_type=MESH)
        return carry

    lax.fori_loop(1, key_n, greet_keys, 0)
    lax.fori_loop(1, row_n, greet_rows, 0)

    lane_k = lax.broadcasted_iota(jnp.int32, (LANES, LANES), 1)
    sub_k = lax.broadcasted_iota(jnp.int32, (LANES, LANES), 0)
    ones = jnp.where(lane_k // HEAD == sub_k // KEYS, 1.0, 0.0).astype(BF16)

    def put_ones(i, carry):
        for g in range(groups):
            v_s[i, g * LANES : (g + 1) * LANES, LANES:] = ones
        return carry

    lax.fori_loop(0, per, put_ones, 0)
    pl.semaphore_wait(barrier, key_n - 1 + row_n - 1)

    def remote(src, dst, send, recv, device):
        return pltpu.make_async_remote_copy(
            src_ref=src, dst_ref=dst, send_sem=send, recv_sem=recv,
            device_id=device, device_id_type=MESH,
        )

    def col_slice(which):
        return pl.ds(pl.multiple_of(which * cols_t, cols_t), cols_t)

    def row_slice(which):
        return pl.ds(pl.multiple_of(which * rows_t, rows_t), rows_t)

    def send_a1(o, carry):
        to = lax.rem(c + o, key_n)
        remote(x_ref.at[pl.ds(to * per, per)], x1.at[:, col_slice(c)], a1_send.at[o], a1_recv.at[o], (r, to)).start()
        return carry

    def wait_a1(o, carry):
        to = lax.rem(c + key_n - o, key_n)
        copy = remote(x_ref.at[pl.ds(to * per, per)], x1.at[:, col_slice(to)], a1_send.at[o], a1_recv.at[o], (r, to))
        copy.wait_send()
        copy.wait_recv()
        return carry

    def gather_start(buf, send, recv):
        sends = []
        for d in range(1, y_n):
            to = lax.rem(y + d, y_n)
            own = buf.at[y, core, z, xx]
            copy = remote(own, own, send.at[d], recv.at[d], (to * 2 + core, c))
            copy.start()
            sends.append(copy)
        return sends

    def gather_plan(buf, send, recv):
        base = y_n
        n1 = z_n - 1
        mate = (y * 2 + 1 - core, c)

        def zdev(d):
            return (r, lax.rem(z + d, z_n) * x_n + xx)

        def xdev(d):
            return (r, z * x_n + lax.rem(xx + d, x_n))

        def zoff(d):
            return lax.rem(z + z_n - d, z_n)

        def xoff(d):
            return lax.rem(xx + x_n - d, x_n)

        low, high = slice(0, y_h), slice(y_h, y_n)
        s1_in = [remote(buf.at[lax.rem(y + y_n - d, y_n), core, z, xx], buf.at[lax.rem(y + y_n - d, y_n), core, z, xx],
                        send.at[d], recv.at[d], (lax.rem(y + y_n - d, y_n) * 2 + core, c)) for d in range(1, y_n)]
        s2_out, s2_in, s3_out, s3_in = [], [], [], []
        m2, m3 = [], []

        def both(ref, slot, device, outs):
            outs.append(remote(ref, ref, send.at[slot], recv.at[slot], device))

        slot = base
        for d in range(1, z_n):
            both(buf.at[low, core, z, xx], slot, zdev(d), s2_out)
            both(buf.at[low, core, zoff(d), xx], slot, zdev(z_n - d), s2_in)
            slot += 1
            both(buf.at[high, core, z, xx], slot, xdev(d), s2_out)
            both(buf.at[high, core, z, xoff(d)], slot, xdev(x_n - d), s2_in)
            slot += 1
        for d in range(1, z_n):
            both(buf.at[low, core, :, xx], slot, xdev(d), s3_out)
            both(buf.at[low, core, :, xoff(d)], slot, xdev(x_n - d), s3_in)
            slot += 1
            both(buf.at[high, core, z, :], slot, zdev(d), s3_out)
            both(buf.at[high, core, zoff(d), :], slot, zdev(z_n - d), s3_in)
            slot += 1
        m_out, m_in = [], []
        both(buf.at[:, core, z, xx], slot, mate, m_out)
        both(buf.at[:, 1 - core, z, xx], slot, mate, m_in)
        slot += 1
        for d in range(1, z_n):
            both(buf.at[low, core, zoff(d), xx], slot, mate, m_out)
            both(buf.at[low, 1 - core, zoff(d), xx], slot, mate, m_in)
            slot += 1
            both(buf.at[high, core, z, xoff(d)], slot, mate, m_out)
            both(buf.at[high, 1 - core, z, xoff(d)], slot, mate, m_in)
            slot += 1
        for d in range(1, z_n):
            both(buf.at[low, core, :, xoff(d)], slot, mate, m_out)
            both(buf.at[low, 1 - core, :, xoff(d)], slot, mate, m_in)
            slot += 1
            both(buf.at[high, core, zoff(d), :], slot, mate, m_out)
            both(buf.at[high, 1 - core, zoff(d), :], slot, mate, m_in)
            slot += 1
        return s1_in, s2_out, s2_in, s3_out, s3_in, m_out, m_in

    def start_all(copies):
        for copy in copies:
            copy.start()

    lane_q = lax.broadcasted_iota(jnp.int32, (KEYS, LANES), 1)

    def prepare(m, xs, i):
        normed = layer_norm(xs[i].astype(F32), gain_ref[m], shift_ref[m]).astype(BF16)

        def project(part):
            return jnp.dot(normed, wp_ref[m, :, part * LANES : (part + 1) * LANES], preferred_element_type=F32)

        q_s[i] = (project(0) * HEAD**-0.5).astype(BF16)
        k = project(1).astype(BF16)
        v = project(2).astype(BF16)
        g_s[i] = jax.nn.sigmoid(project(3) + gb_ref[m])
        for g in range(groups):
            kg = k[g * KEYS : (g + 1) * KEYS]
            vg = v[g * KEYS : (g + 1) * KEYS]
            for h in range(HEADS):
                mine = lane_q // HEAD == h
                at = g * LANES + h * KEYS
                k_s[i, at : at + KEYS, :] = jnp.where(mine, kg, jnp.zeros_like(kg))
                v_s[i, at : at + KEYS, :LANES] = jnp.where(mine, vg, jnp.zeros_like(vg))

    def attend(m, i):
        width = groups * LANES
        q = q_s[i]
        top = None
        for n in range(0, width, CHUNK):
            s = lax.dot_general(q, k_s[i, n : n + CHUNK, :], (((1,), (1,)), ((), ())), preferred_element_type=F32)
            s = s + bias_s[:, n : n + CHUNK]
            s_s[:, n : n + CHUNK] = s
            for t in range(0, CHUNK, LANES):
                part = s[:, t : t + LANES]
                top = part if top is None else jnp.maximum(top, part)
        top = head_max(top, lane)
        top = jnp.concatenate([top] * (CHUNK // LANES), axis=1)
        total = jnp.zeros((tokens, 2 * LANES), F32)
        for n in range(0, width, CHUNK):
            p = jnp.exp2((s_s[:, n : n + CHUNK] - top) * LOG2E).astype(BF16)
            total = total + jnp.dot(p, v_s[i, n : n + CHUNK, :], preferred_element_type=F32)
        gated = (total[:, :LANES] / total[:, LANES:] * g_s[i]).astype(BF16)
        return jnp.dot(gated, wo_ref[m], preferred_element_type=F32)

    lax.fori_loop(1, key_n, send_a1, 0)
    x1[:, col_slice(c)] = x_ref[pl.ds(c * per, per)]

    tile_f[...] = layer_norm(x_ref[...].astype(F32), gain_ref[0], shift_ref[0])

    def pick(m, k):
        return jnp.where(lane_k % KEYS == k, wb_ref[m], jnp.zeros((LANES, LANES), BF16))

    acc = jnp.zeros((rows_t, LANES), F32)
    for k in range(0, cols_t, 2):
        left = jnp.concatenate([tile_f[:, k, :], tile_f[:, k + 1, :]], axis=1).astype(BF16)
        right = jnp.concatenate([pick(0, k), pick(0, k + 1)], axis=0)
        acc = acc + jnp.dot(left, right, preferred_element_type=F32)
    bias_a[y, core, z, xx] = acc.astype(BF16)

    def run_gather(buf, send, recv, work):
        s1_out = gather_start(buf, send, recv)
        s1_in, s2_out, s2_in, s3_out, s3_in, m_out, m_in = gather_plan(buf, send, recv)
        n1 = 2 * (z_n - 1)
        for copy in s1_in:
            copy.wait_recv()
        start_all(s2_out)
        m_out[0].start()
        work[0]()
        for copy in s2_in:
            copy.wait_recv()
        start_all(s3_out)
        start_all(m_out[1 : 1 + n1])
        work[1]()
        for arrived, onward in zip(s3_in, m_out[1 + n1 :]):
            arrived.wait_recv()
            onward.start()
        work[2]()
        for copy in m_in:
            copy.wait_recv()
        for copy in s1_out + s2_out + s3_out + m_out:
            copy.wait_send()

    def first_rows():
        lax.fori_loop(1, key_n, wait_a1, 0)
        prepare(0, x1, 0)

    def more(m, xs, lo, hi):
        def one(i, carry):
            prepare(m, xs, i)
            return carry

        lax.fori_loop(lo, hi, one, 0)

    run_gather(bias_a, ga_send, ga_recv, [first_rows, lambda: more(0, x1, 1, per), lambda: None])

    for yy in range(y_n):
        for cc in range(2):
            def widen(g, carry, yy=yy, cc=cc):
                at = pl.ds(pl.multiple_of(g * LANES, LANES), LANES)
                block = bias_a[yy, cc, g // x_n, g % x_n].astype(F32)
                rr = yy * 2 + cc
                bias_s[rr * rows_t : (rr + 1) * rows_t, at] = block + kb_ref[pl.ds(g, 1), :]
                return carry

            lax.fori_loop(0, key_n, widen, 0)

    def a2_copy(i, n, o, to, frm):
        return remote(
            as1.at[pl.ds(i, n), col_slice(to)], t2.at[pl.ds(frm * per + i, n)], a2_send.at[o], a2_recv.at[o], (r, to)
        )

    def row_one(i, carry):
        update = attend(0, i)
        keep = mk_ref[pl.ds(rows_t * r + per * c + i, 1), :] * mk_ref[...]
        as1[i] = (x1[i].astype(F32) + keep * update).astype(BF16)

        def send(o, inner):
            to = lax.rem(c + o, key_n)
            a2_copy(i, 1, o, to, c).start()
            return inner

        lax.fori_loop(1, key_n, send, 0)
        t2[per * c + i] = as1[i, col_slice(c)]
        return carry

    lax.fori_loop(0, per, row_one, 0)

    def wait_a2(o, carry):
        a2_copy(0, per, o, lax.rem(c + o, key_n), c).wait_send()
        frm = lax.rem(c + key_n - o, key_n)
        a2_copy(0, per, o, frm, frm).wait_recv()
        return carry

    lax.fori_loop(1, key_n, wait_a2, 0)

    tile_f[...] = t2[...].astype(F32)
    for j in range(cols_t):
        sb[j] = tile_f[:, j, :].astype(BF16)

    def b2_copy(o, to, frm):
        return remote(sb.at[pl.ds(to * per, per)], x2.at[:, row_slice(frm)], b2_send.at[o], b2_recv.at[o], (to, c))

    def send_b2(o, carry):
        b2_copy(o, lax.rem(r + o, row_n), r).start()
        return carry

    def wait_b2(o, carry):
        b2_copy(o, lax.rem(r + o, row_n), r).wait_send()
        frm = lax.rem(r + row_n - o, row_n)
        b2_copy(o, frm, frm).wait_recv()
        return carry

    lax.fori_loop(1, row_n, send_b2, 0)
    x2[:, row_slice(r)] = sb[pl.ds(r * per, per)]

    tile_f[...] = layer_norm(tile_f[...], gain_ref[1], shift_ref[1])
    halves = rows_t // KEYS

    acc = jnp.zeros((rows_t, LANES), F32)
    for k in range(0, KEYS, 2):
        left = jnp.concatenate(
            [jnp.concatenate([tile_f[h * KEYS + kk] for h in range(halves)], axis=0) for kk in (k, k + 1)], axis=1
        ).astype(BF16)
        right = jnp.concatenate([pick(1, k), pick(1, k + 1)], axis=0)
        acc = acc + jnp.dot(left, right, preferred_element_type=F32)
    bias_b[y, core, z, xx] = acc.astype(BF16)

    def second_rows():
        lax.fori_loop(1, row_n, wait_b2, 0)
        prepare(1, x2, 0)

    run_gather(bias_b, gb_send, gb_recv, [second_rows, lambda: more(1, x2, 1, per), lambda: None])

    for yy in range(y_n):
        for cc in range(2):
            for h in range(halves):
                def widen_two(g, carry, yy=yy, cc=cc, h=h):
                    lane_at = ((yy * 2 + cc) * halves + h)
                    block = bias_b[yy, cc, g // x_n, g % x_n, h * KEYS : (h + 1) * KEYS, :].astype(F32)
                    bias_s[col_slice(g), lane_at * LANES : (lane_at + 1) * LANES] = (
                        block + kb_ref[lane_at : lane_at + 1, :]
                    )
                    return carry

                lax.fori_loop(0, key_n, widen_two, 0)

    def c2_copy(i, n, o, to, frm):
        return remote(
            np2.at[pl.ds(i, n), row_slice(to)], fin.at[pl.ds(frm * per + i, n)], c2_send.at[o], c2_recv.at[o], (to, c)
        )

    def row_two(i, carry):
        update = attend(1, i)
        keep = mk_ref[pl.ds(cols_t * c + per * r + i, 1), :] * mk_ref[...]
        update = (keep * update).astype(BF16).astype(F32)
        np2[i] = (x2[i].astype(F32) + update).astype(BF16)

        def send(o, inner):
            c2_copy(i, 1, o, lax.rem(r + o, row_n), r).start()
            return inner

        lax.fori_loop(1, row_n, send, 0)
        fin[per * r + i] = np2[i, row_slice(r)]
        return carry

    lax.fori_loop(0, per, row_two, 0)

    def wait_c2(o, carry):
        c2_copy(0, per, o, lax.rem(r + o, row_n), r).wait_send()
        frm = lax.rem(r + row_n - o, row_n)
        c2_copy(0, per, o, frm, frm).wait_recv()
        return carry

    lax.fori_loop(1, row_n, wait_c2, 0)
    for j in range(cols_t):
        tile_f[:, j, :] = fin[j].astype(F32)
    out_ref[...] = tile_f[...].astype(BF16)


def local(row_n, key_n, pair_rep, token_mask, norm_gain, norm_shift, w_proj, w_bias, gate_bias, w_out):
    rows_t, cols_t, channels = pair_rep.shape
    tokens = token_mask.shape[0]
    per = tokens // (row_n * key_n)
    groups = tokens // KEYS
    width = groups * LANES
    mask = token_mask.astype(F32)
    key_bias = (mask - 1.0) * 1000000000.0
    kb = jnp.tile(key_bias.reshape(groups, 1, KEYS), (1, HEADS, 1)).reshape(groups, LANES)
    mk = jnp.broadcast_to(mask[:, None], (tokens, LANES))
    wb = jnp.repeat(w_bias, KEYS, axis=2)
    y_n, z_n = row_n // 2, int(round(key_n**0.5))
    slots = y_n + 4 * (z_n - 1) + 1 + 4 * (z_n - 1)
    vmem, dma = pltpu.VMEM, pltpu.SemaphoreType.DMA
    buf = (y_n, 2, z_n, z_n, rows_t, LANES)
    return pl.pallas_call(
        functools.partial(kernel, tokens, row_n, key_n),
        out_shape=jax.ShapeDtypeStruct(pair_rep.shape, BF16),
        in_specs=[pl.BlockSpec(memory_space=pltpu.VMEM)] * 9,
        out_specs=pl.BlockSpec(memory_space=pltpu.VMEM),
        scratch_shapes=[
            vmem((per, tokens, LANES), BF16),
            vmem((per, tokens, LANES), BF16),
            vmem((per, tokens, LANES), BF16),
            vmem((per, tokens, LANES), BF16),
            vmem((rows_t, cols_t, LANES), BF16),
            vmem((cols_t, rows_t, LANES), BF16),
            vmem((cols_t, rows_t, LANES), BF16),
            vmem((rows_t, cols_t, LANES), F32),
            vmem(buf, BF16),
            vmem(buf, BF16),
            vmem((tokens, width), F32),
            vmem((per, tokens, LANES), BF16),
            vmem((per, width, LANES), BF16),
            vmem((per, width, 2 * LANES), BF16),
            vmem((per, tokens, LANES), F32),
            vmem((tokens, width), F32),
            dma((key_n,)), dma((key_n,)), dma((key_n,)), dma((key_n,)),
            dma((row_n,)), dma((row_n,)), dma((row_n,)), dma((row_n,)),
            dma((slots,)), dma((slots,)), dma((slots,)), dma((slots,)),
        ],
        compiler_params=pltpu.CompilerParams(
            collective_id=0, has_side_effects=True, vmem_limit_bytes=56 * 2**20
        ),
        name="triangle_attention",
    )(
        pair_rep, kb, mk, norm_gain[:, None, :], norm_shift[:, None, :], w_proj, wb,
        gate_bias[:, None, :], w_out,
    )


def solution(mesh):
    row_n, key_n = mesh.shape["rows"], mesh.shape["keys"]
    in_specs = (P("rows", "keys", None), P(), P(), P(), P(), P(), P(), P())
    out_specs = P("rows", "keys", None)
    return jax.shard_map(
        functools.partial(local, row_n, key_n), mesh=mesh, in_specs=in_specs, out_specs=out_specs, check_vma=False
    )
```

```python
import functools

import jax
import jax.numpy as jnp
from jax import lax
from jax.experimental import pallas as pl
from jax.experimental.pallas import tpu as pltpu
from jax.sharding import PartitionSpec as P

MESH = pl.DeviceIdType.MESH
LOG2E = 1.4426950408889634
F32 = jnp.float32
BF16 = jnp.bfloat16
KEYS = 32
HEADS = 4
HEAD = 32
LANES = 128
CHUNK = 256


def layer_norm(values, gain, shift):
    center = jnp.mean(values, axis=-1, keepdims=True)
    moved = values - center
    spread = jnp.mean(moved * moved, axis=-1, keepdims=True)
    return moved * lax.rsqrt(spread + 1e-05) * gain + shift


def head_max(m, lane):
    for step in (16, 8, 4, 2, 1):
        below = pltpu.roll(m, step, 1)
        above = pltpu.roll(m, LANES - step, 1)
        m = jnp.maximum(m, jnp.where((lane & step) != 0, below, above))
    return m


def kernel(
    tokens, row_n, key_n,
    x_ref, mask_ref, gain_ref, shift_ref, wp_ref, wb_ref, gb_ref, wo_ref,
    out_ref,
    x1, x2, as1, np2, t2, sb, fin, tile_f, bias_a, bias_b, bias_s, q_s, k_s, v_s, g_s,
    s_even, s_odd, p_even, p_odd, top_s, wr_s,
    a1_send, a1_recv, a2_send, a2_recv, b2_send, b2_recv, c2_send, c2_recv,
    ga_send, ga_recv, gb_send, gb_recv,
):
    rows_t, cols_t = tokens // row_n, tokens // key_n
    per = tokens // (row_n * key_n)
    groups = tokens // KEYS
    y_n = row_n // 2
    z_n = x_n = int(round(key_n**0.5))
    half_t = tokens // 2
    r, c = lax.axis_index("rows"), lax.axis_index("keys")
    y, core = r // 2, r % 2
    z, xx = c // x_n, c % x_n
    lane = lax.broadcasted_iota(jnp.int32, (1, LANES), 1)

    barrier = pltpu.get_barrier_semaphore()

    def greet_keys(o, carry):
        pl.semaphore_signal(barrier, inc=1, device_id=(r, lax.rem(c + o, key_n)), device_id_type=MESH)
        return carry

    def greet_rows(o, carry):
        pl.semaphore_signal(barrier, inc=1, device_id=(lax.rem(r + o, row_n), c), device_id_type=MESH)
        return carry

    lax.fori_loop(1, key_n, greet_keys, 0)
    lax.fori_loop(1, row_n, greet_rows, 0)

    real = jnp.sum(mask_ref[...], keepdims=True)

    def key_bias(g):
        key = g * KEYS + lane % KEYS
        return jnp.where(key < real, 0.0, -1000000000.0)

    def kept(first, token, count):
        at = first + lax.broadcasted_iota(jnp.int32, (count, LANES), 0)
        return jnp.where(jnp.logical_and(at < real, token < real), 1.0, 0.0)

    lane_k = lax.broadcasted_iota(jnp.int32, (LANES, LANES), 1)
    sub_k = lax.broadcasted_iota(jnp.int32, (LANES, LANES), 0)
    ones = jnp.where(lane_k // HEAD == sub_k // KEYS, 1.0, 0.0).astype(BF16)

    def put_ones(i, carry):
        for g in range(groups):
            v_s[i, g * LANES : (g + 1) * LANES, LANES:] = ones
        return carry

    lax.fori_loop(0, per, put_ones, 0)
    spread = lax.broadcasted_iota(jnp.int32, (HEADS, LANES), 0) == lax.broadcasted_iota(jnp.int32, (HEADS, LANES), 1) // KEYS
    spread = jnp.where(spread, 1.0, 0.0).astype(BF16)
    for m in range(2):
        wr_s[m] = jnp.dot(wb_ref[m], spread, preferred_element_type=F32).astype(BF16)
    pl.semaphore_wait(barrier, key_n - 1 + row_n - 1)

    def remote(src, dst, send, recv, device):
        return pltpu.make_async_remote_copy(
            src_ref=src, dst_ref=dst, send_sem=send, recv_sem=recv,
            device_id=device, device_id_type=MESH,
        )

    def col_slice(which):
        return pl.ds(pl.multiple_of(which * cols_t, cols_t), cols_t)

    def row_slice(which):
        return pl.ds(pl.multiple_of(which * rows_t, rows_t), rows_t)

    def send_a1(o, carry):
        to = lax.rem(c + o, key_n)
        remote(x_ref.at[pl.ds(to * per, per)], x1.at[:, col_slice(c)], a1_send.at[o], a1_recv.at[o], (r, to)).start()
        return carry

    def wait_a1(o, carry):
        to = lax.rem(c + key_n - o, key_n)
        copy = remote(x_ref.at[pl.ds(to * per, per)], x1.at[:, col_slice(to)], a1_send.at[o], a1_recv.at[o], (r, to))
        copy.wait_send()
        copy.wait_recv()
        return carry

    size = {"y": y_n, "z": z_n, "x": x_n}
    place = {"y": y, "z": z, "x": xx}

    def device(which_core, **at):
        at = {**place, **at}
        return (at["y"] * 2 + which_core, at["z"] * x_n + at["x"])

    def shifted(axis, d):
        return lax.rem(place[axis] + d, size[axis])

    class Gather:
        def __init__(self, buf, send, recv, axes):
            self.buf, self.send, self.recv = buf, send, recv
            self.first, self.others = axes[0], axes[1:]
            self.parts = size[axes[0]]
            self.turns = size[axes[1]] - 1

        def block(self, which_core, **at):
            at = {**place, **at}
            return self.buf.at[at["y"], which_core, at["z"], at["x"]]

        def copy(self, slot, ref, to):
            return remote(ref, ref, self.send.at[slot], self.recv.at[slot], to)

        def line(self, p, which_core, **at):
            u, v = self.others if p % 2 == 0 else self.others[::-1]
            return self.block(which_core, **{self.first: p, u: slice(None), v: at.get("v", place[v])})

        def one(self, d, out):
            near = shifted(self.first, size[self.first] - d)
            if out:
                return self.copy(d - 1, self.block(core), device(core, **{self.first: shifted(self.first, d)}))
            return self.copy(d - 1, self.block(core, **{self.first: near}), device(core, **{self.first: near}))

        def two(self, p, d, out):
            u = self.others[p % 2]
            slot = self.parts - 1 + p * self.turns + d - 1
            near = shifted(u, size[u] - d)
            if out:
                return self.copy(slot, self.block(core, **{self.first: p}), device(core, **{u: shifted(u, d)}))
            return self.copy(slot, self.block(core, **{self.first: p, u: near}), device(core, **{u: near}))

        def three(self, p, d, out):
            v = self.others[1 - p % 2]
            slot = self.parts - 1 + (self.parts + p) * self.turns + d - 1
            near = shifted(v, size[v] - d)
            if out:
                return self.copy(slot, self.line(p, core), device(core, **{v: shifted(v, d)}))
            return self.copy(slot, self.line(p, core, v=near), device(core, **{v: near}))

        def mate(self, p, d, out):
            v = self.others[1 - p % 2]
            slot = self.parts - 1 + 2 * self.parts * self.turns + p * (self.turns + 1) + d
            near = shifted(v, size[v] - d)
            return self.copy(slot, self.line(p, core if out else 1 - core, v=near), device(1 - core))

        def steps(self):
            return range(1, self.turns + 1)

        def start_one(self):
            for d in range(1, self.parts):
                self.one(d, True).start()

        def start_two(self):
            for d in range(1, self.parts):
                self.one(d, False).wait_recv()
            for p in range(self.parts):
                for d in self.steps():
                    self.two(p, d, True).start()

        def half(self, h):
            return range(h * self.parts // 2, (h + 1) * self.parts // 2)

        def start_three(self, h):
            for p in self.half(h):
                for d in self.steps():
                    self.two(p, d, False).wait_recv()
                for d in self.steps():
                    self.three(p, d, True).start()
                self.mate(p, 0, True).start()

        def pass_on(self, h):
            for d in self.steps():
                for p in self.half(h):
                    self.three(p, d, False).wait_recv()
                    self.mate(p, d, True).start()

        def finish(self, h):
            for p in self.half(h):
                for d in range(self.turns + 1):
                    self.mate(p, d, False).wait_recv()

        def drain(self):
            for d in range(1, self.parts):
                self.one(d, True).wait_send()
            for p in range(self.parts):
                for d in self.steps():
                    self.two(p, d, True).wait_send()
                    self.three(p, d, True).wait_send()
                for d in range(self.turns + 1):
                    self.mate(p, d, True).wait_send()

    lane_q = lax.broadcasted_iota(jnp.int32, (KEYS, LANES), 1)

    def prepare(m, xs, i):
        normed = layer_norm(xs[i].astype(F32), gain_ref[m : m + 1], shift_ref[m : m + 1]).astype(BF16)

        def project(part):
            return jnp.dot(normed, wp_ref[m, :, part * LANES : (part + 1) * LANES], preferred_element_type=F32)

        q_s[i] = (project(0) * HEAD**-0.5).astype(BF16)
        k = project(1).astype(BF16)
        v = project(2).astype(BF16)
        g_s[i] = jax.nn.sigmoid(project(3) + gb_ref[m : m + 1])
        for g in range(groups):
            kg = k[g * KEYS : (g + 1) * KEYS]
            vg = v[g * KEYS : (g + 1) * KEYS]
            for h in range(HEADS):
                mine = lane_q // HEAD == h
                at = g * LANES + h * KEYS
                k_s[i, at : at + KEYS, :] = jnp.where(mine, kg, jnp.zeros_like(kg))
                v_s[i, at : at + KEYS, :LANES] = jnp.where(mine, vg, jnp.zeros_like(vg))

    width = groups * LANES

    def score_chunk(row, at, s_s, n, top):
        s = lax.dot_general(
            q_s[row, at, :], k_s[row, n : n + CHUNK, :], (((1,), (1,)), ((), ())), preferred_element_type=F32
        )
        s = s + bias_s[at, n : n + CHUNK]
        s_s[:, n : n + CHUNK] = s
        for t in range(0, CHUNK, LANES):
            part = s[:, t : t + LANES]
            top = part if top is None else jnp.maximum(top, part)
        return top

    def weight_chunk(s_s, p_s, n, top):
        p_s[:, n : n + CHUNK] = jnp.exp2((s_s[:, n : n + CHUNK] - top) * LOG2E).astype(BF16)

    def attend(m, unit_done, between):
        units = 2 * per

        def where(unit):
            return lax.rem(unit, per), pl.ds(pl.multiple_of(unit // per * half_t, half_t), half_t)

        def scores(unit, s_s, slot, before=None):
            row, at = where(unit)
            top = None
            if before is not None:
                s_b, p_b, slot_b = before
                top_b = jnp.concatenate([top_s[slot_b]] * (CHUNK // LANES), axis=1)
            for n in range(0, width, CHUNK):
                if before is not None:
                    weight_chunk(s_b, p_b, n, top_b)
                top = score_chunk(row, at, s_s, n, top)
            top_s[slot] = head_max(top, lane)

        def weights(s_s, p_s, slot):
            top = jnp.concatenate([top_s[slot]] * (CHUNK // LANES), axis=1)
            for n in range(0, width, CHUNK):
                weight_chunk(s_s, p_s, n, top)

        def values(unit, p_s):
            row, at = where(unit)
            total = jnp.dot(p_s[...], v_s[row], preferred_element_type=F32)
            gated = (total[:, :LANES] / total[:, LANES:] * g_s[row, at, :]).astype(BF16)
            update = jnp.dot(gated, wo_ref[m], preferred_element_type=F32)
            unit_done(row, unit // per, at, update)

        scores(0, s_even, 0)

        def pair(t, carry):
            unit = 2 * t
            scores(unit + 1, s_odd, 1, (s_even, p_even, 0))
            values(unit, p_even)

            @pl.when(t == per // 2 - 1)
            def _():
                between()

            @pl.when(t < per - 1)
            def _():
                scores(unit + 2, s_even, 0, (s_odd, p_odd, 1))
                values(unit + 1, p_odd)

            @pl.when(t == per - 1)
            def _():
                weights(s_odd, p_odd, 1)
                values(unit + 1, p_odd)

            return carry

        lax.fori_loop(0, per, pair, 0)

    lax.fori_loop(1, key_n, send_a1, 0)
    x1[:, col_slice(c)] = x_ref[pl.ds(c * per, per)]

    tile_f[...] = layer_norm(x_ref[...].astype(F32), gain_ref[0:1], shift_ref[0:1])

    def pick(m, k):
        return jnp.where(lane_k % KEYS == k, wr_s[m], jnp.zeros((LANES, LANES), BF16))

    acc = jnp.zeros((rows_t, LANES), F32)
    for k in range(0, cols_t, 2):
        left = jnp.concatenate([tile_f[:, k, :], tile_f[:, k + 1, :]], axis=1).astype(BF16)
        right = jnp.concatenate([pick(0, k), pick(0, k + 1)], axis=0)
        acc = acc + jnp.dot(left, right, preferred_element_type=F32)
    bias_a[y, core, z, xx] = acc.astype(BF16)

    def more(m, xs, lo, hi):
        def one(i, carry):
            prepare(m, xs, i)
            return carry

        lax.fori_loop(lo, hi, one, 0)

    def widen_one(h):
        def widen(g, carry):
            at = pl.ds(pl.multiple_of(g * LANES, LANES), LANES)
            masked = key_bias(g)
            for rr in range(h * row_n // 2, (h + 1) * row_n // 2):
                block = bias_a[rr // 2, rr % 2, g // x_n, lax.rem(g, x_n)].astype(F32)
                bias_s[rr * rows_t : (rr + 1) * rows_t, at] = block + masked
            return carry

        lax.fori_loop(0, key_n, widen, 0)

    moves = Gather(bias_a, ga_send, ga_recv, "yzx")
    moves.start_one()
    moves.start_two()
    lax.fori_loop(1, key_n, wait_a1, 0)
    more(0, x1, 0, 1)
    moves.start_three(0)
    moves.start_three(1)
    more(0, x1, 1, per)
    moves.pass_on(0)
    moves.finish(0)
    widen_one(0)

    def a2_copy(i, n, to, frm):
        return remote(
            as1.at[pl.ds(i, n), col_slice(to)], t2.at[pl.ds(frm * per + i, n)], a2_send.at[to], a2_recv.at[frm], (r, to)
        )

    def unit_one(i, h, at, update):
        keep = kept(h * half_t, rows_t * r + per * c + i, half_t)
        as1[i, at, :] = (x1[i, at, :].astype(F32) + keep * update).astype(BF16)

        def send(o, inner):
            to = h * (key_n // 2) + lax.rem(c + o, key_n // 2)

            @pl.when(to != c)
            def _():
                a2_copy(i, 1, to, c).start()

            return inner

        lax.fori_loop(0, key_n // 2, send, 0)

    def between_one():
        moves.pass_on(1)
        moves.finish(1)
        widen_one(1)

    attend(0, unit_one, between_one)
    t2[pl.ds(per * c, per)] = as1[:, col_slice(c)]
    moves.drain()

    def wait_a2(o, carry):
        to = lax.rem(c + o, key_n)
        a2_copy(0, per, to, c).wait_send()
        frm = lax.rem(c + key_n - o, key_n)
        copy = remote(
            as1.at[pl.ds(0, per), col_slice(c)], t2.at[pl.ds(frm * per, per)], a2_send.at[frm], a2_recv.at[frm], (r, frm)
        )
        copy.wait_recv()
        return carry

    lax.fori_loop(1, key_n, wait_a2, 0)

    tile_f[...] = t2[...].astype(F32)
    for j in range(cols_t):
        sb[j] = tile_f[:, j, :].astype(BF16)

    def b2_copy(o, to, frm):
        return remote(sb.at[pl.ds(to * per, per)], x2.at[:, row_slice(frm)], b2_send.at[o], b2_recv.at[o], (to, c))

    def send_b2(o, carry):
        b2_copy(o, lax.rem(r + o, row_n), r).start()
        return carry

    def wait_b2(o, carry):
        b2_copy(o, lax.rem(r + o, row_n), r).wait_send()
        frm = lax.rem(r + row_n - o, row_n)
        b2_copy(o, frm, frm).wait_recv()
        return carry

    tile_f[...] = layer_norm(tile_f[...], gain_ref[1:2], shift_ref[1:2])
    halves = rows_t // KEYS

    acc = jnp.zeros((rows_t, LANES), F32)
    for k in range(0, KEYS, 2):
        left = jnp.concatenate(
            [jnp.concatenate([tile_f[h * KEYS + kk] for h in range(halves)], axis=0) for kk in (k, k + 1)], axis=1
        ).astype(BF16)
        right = jnp.concatenate([pick(1, k), pick(1, k + 1)], axis=0)
        acc = acc + jnp.dot(left, right, preferred_element_type=F32)
    bias_b[y, core, z, xx] = acc.astype(BF16)

    moves_two = Gather(bias_b, gb_send, gb_recv, "zyx")
    moves_two.start_one()
    lax.fori_loop(1, row_n, send_b2, 0)
    x2[:, row_slice(r)] = sb[pl.ds(r * per, per)]
    moves_two.start_two()
    lax.fori_loop(1, row_n, wait_b2, 0)
    more(1, x2, 0, 1)
    moves_two.start_three(0)
    moves_two.start_three(1)
    more(1, x2, 1, per)
    moves_two.pass_on(0)
    moves_two.finish(0)

    def widen_two(h):
        def widen(g, carry):
            for gg in range(row_n * halves):
                rr, hh = gg // halves, gg % halves
                block = bias_b[rr // 2, rr % 2, g // x_n, lax.rem(g, x_n), hh * KEYS : (hh + 1) * KEYS, :].astype(F32)
                bias_s[col_slice(g), gg * LANES : (gg + 1) * LANES] = block + key_bias(gg)
            return carry

        lax.fori_loop(h * key_n // 2, (h + 1) * key_n // 2, widen, 0)

    widen_two(0)

    def c2_copy(i, n, to, frm):
        return remote(
            np2.at[pl.ds(i, n), row_slice(to)], fin.at[pl.ds(frm * per + i, n)], c2_send.at[to], c2_recv.at[frm], (to, c)
        )

    def unit_two(i, h, at, update):
        keep = kept(h * half_t, cols_t * c + per * r + i, half_t)
        update = (keep * update).astype(BF16).astype(F32)
        np2[i, at, :] = (x2[i, at, :].astype(F32) + update).astype(BF16)

        def send(o, inner):
            to = h * (row_n // 2) + lax.rem(r + o, row_n // 2)

            @pl.when(to != r)
            def _():
                c2_copy(i, 1, to, r).start()

            return inner

        lax.fori_loop(0, row_n // 2, send, 0)

    def between_two():
        moves_two.pass_on(1)
        moves_two.finish(1)
        widen_two(1)

    attend(1, unit_two, between_two)
    fin[pl.ds(per * r, per)] = np2[:, row_slice(r)]
    moves_two.drain()

    def wait_c2(o, carry):
        c2_copy(0, per, lax.rem(r + o, row_n), r).wait_send()
        frm = lax.rem(r + row_n - o, row_n)
        copy = remote(
            np2.at[pl.ds(0, per), row_slice(r)], fin.at[pl.ds(frm * per, per)], c2_send.at[frm], c2_recv.at[frm], (frm, c)
        )
        copy.wait_recv()
        return carry

    lax.fori_loop(1, row_n, wait_c2, 0)
    for j in range(cols_t):
        tile_f[:, j, :] = fin[j].astype(F32)
    out_ref[...] = tile_f[...].astype(BF16)


def local(row_n, key_n, pair_rep, token_mask, norm_gain, norm_shift, w_proj, w_bias, gate_bias, w_out):
    rows_t, cols_t, channels = pair_rep.shape
    tokens = token_mask.shape[0]
    per = tokens // (row_n * key_n)
    groups = tokens // KEYS
    width = groups * LANES
    y_n, z_n = row_n // 2, int(round(key_n**0.5))
    slots = y_n - 1 + 2 * y_n * (z_n - 1) + y_n * z_n
    vmem, dma = pltpu.VMEM, pltpu.SemaphoreType.DMA
    buf = (y_n, 2, z_n, z_n, rows_t, LANES)
    return pl.pallas_call(
        functools.partial(kernel, tokens, row_n, key_n),
        out_shape=jax.ShapeDtypeStruct(pair_rep.shape, BF16),
        in_specs=[pl.BlockSpec(memory_space=pltpu.VMEM)] * 8,
        out_specs=pl.BlockSpec(memory_space=pltpu.VMEM),
        scratch_shapes=[
            vmem((per, tokens, LANES), BF16),
            vmem((per, tokens, LANES), BF16),
            vmem((per, tokens, LANES), BF16),
            vmem((per, tokens, LANES), BF16),
            vmem((rows_t, cols_t, LANES), BF16),
            vmem((cols_t, rows_t, LANES), BF16),
            vmem((cols_t, rows_t, LANES), BF16),
            vmem((rows_t, cols_t, LANES), F32),
            vmem(buf, BF16),
            vmem(buf, BF16),
            vmem((tokens, width), F32),
            vmem((per, tokens, LANES), BF16),
            vmem((per, width, LANES), BF16),
            vmem((per, width, 2 * LANES), BF16),
            vmem((per, tokens, LANES), F32),
            vmem((tokens // 2, width), F32),
            vmem((tokens // 2, width), F32),
            vmem((tokens // 2, width), BF16),
            vmem((tokens // 2, width), BF16),
            vmem((2, tokens // 2, LANES), F32),
            vmem((2, LANES, LANES), BF16),
            dma((key_n,)), dma((key_n,)), dma((key_n,)), dma((key_n,)),
            dma((row_n,)), dma((row_n,)), dma((row_n,)), dma((row_n,)),
            dma((slots,)), dma((slots,)), dma((slots,)), dma((slots,)),
        ],
        compiler_params=pltpu.CompilerParams(
            collective_id=0, has_side_effects=True, vmem_limit_bytes=56 * 2**20
        ),
        name="triangle_attention",
    )(
        pair_rep, token_mask.reshape(-1, min(tokens, LANES)), norm_gain, norm_shift, w_proj, w_bias, gate_bias, w_out,
    )


def solution(mesh):
    row_n, key_n = mesh.shape["rows"], mesh.shape["keys"]
    in_specs = (P("rows", "keys", None), P(), P(), P(), P(), P(), P(), P())
    out_specs = P("rows", "keys", None)
    return jax.shard_map(
        functools.partial(local, row_n, key_n), mesh=mesh, in_specs=in_specs, out_specs=out_specs, check_vma=False
    )
```

```python
import functools

import jax
import jax.numpy as jnp
from jax import lax
from jax.experimental import pallas as pl
from jax.experimental.pallas import tpu as pltpu
from jax.sharding import PartitionSpec as P

MESH = pl.DeviceIdType.MESH
LOG2E = 1.4426950408889634
F32 = jnp.float32
BF16 = jnp.bfloat16
KEYS = 32
HEADS = 4
HEAD = 32
LANES = 128
CHUNK = 256


def layer_norm(values, gain, shift):
    center = jnp.mean(values, axis=-1, keepdims=True)
    moved = values - center
    spread = jnp.mean(moved * moved, axis=-1, keepdims=True)
    return moved * lax.rsqrt(spread + 1e-05) * gain + shift


def head_max(m, lane):
    for step in (16, 8, 4, 2, 1):
        below = pltpu.roll(m, step, 1)
        above = pltpu.roll(m, LANES - step, 1)
        m = jnp.maximum(m, jnp.where((lane & step) != 0, below, above))
    return m


def kernel(
    tokens, row_n, key_n,
    x_hbm, mask_ref, gain_ref, shift_ref, wp_ref, wb_ref, gb_ref, wo_ref,
    fin,
    x1, x2, as1, np2, t2, sb, tile_f, bias_a, bias_b, bias_s, q_s, k_s, v_s, g_s,
    s_even, s_odd, p_even, p_odd, top_s, wr_s, x_ref, x_sem,
    a1_send, a1_recv, a2_send, a2_recv, b2_send, b2_recv, c2_send, c2_recv,
    ga_send, ga_recv, gb_send, gb_recv,
):
    rows_t, cols_t = tokens // row_n, tokens // key_n
    per = tokens // (row_n * key_n)
    groups = tokens // KEYS
    y_n = row_n // 2
    z_n = x_n = int(round(key_n**0.5))
    half_t = tokens // 2
    r, c = lax.axis_index("rows"), lax.axis_index("keys")
    y, core = r // 2, r % 2
    z, xx = c // x_n, c % x_n
    lane = lax.broadcasted_iota(jnp.int32, (1, LANES), 1)

    barrier = pltpu.get_barrier_semaphore()
    x_copy = pltpu.make_async_copy(x_hbm, x_ref, x_sem)
    x_copy.start()

    def greet_keys(o, carry):
        pl.semaphore_signal(barrier, inc=1, device_id=(r, lax.rem(c + o, key_n)), device_id_type=MESH)
        return carry

    def greet_rows(o, carry):
        pl.semaphore_signal(barrier, inc=1, device_id=(lax.rem(r + o, row_n), c), device_id_type=MESH)
        return carry

    lax.fori_loop(1, key_n, greet_keys, 0)
    lax.fori_loop(1, row_n, greet_rows, 0)

    real = jnp.sum(mask_ref[...], keepdims=True)

    def key_bias(g):
        key = g * KEYS + lane % KEYS
        return jnp.where(key < real, 0.0, -1000000000.0)

    def kept(first, token, count):
        at = first + lax.broadcasted_iota(jnp.int32, (count, LANES), 0)
        return jnp.where(jnp.logical_and(at < real, token < real), 1.0, 0.0)

    lane_k = lax.broadcasted_iota(jnp.int32, (LANES, LANES), 1)
    sub_k = lax.broadcasted_iota(jnp.int32, (LANES, LANES), 0)
    ones = jnp.where(lane_k // HEAD == sub_k // KEYS, 1.0, 0.0).astype(BF16)

    def put_ones(i, carry):
        for g in range(groups):
            v_s[i, g * LANES : (g + 1) * LANES, LANES:] = ones
        return carry

    lax.fori_loop(0, per, put_ones, 0)
    spread = lax.broadcasted_iota(jnp.int32, (HEADS, LANES), 0) == lax.broadcasted_iota(jnp.int32, (HEADS, LANES), 1) // KEYS
    spread = jnp.where(spread, 1.0, 0.0).astype(BF16)
    for m in range(2):
        wr_s[m] = lax.dot_general(
            wb_ref[m], spread, (((0,), (0,)), ((), ())), preferred_element_type=F32
        ).astype(BF16)
    x_copy.wait()
    pl.semaphore_wait(barrier, key_n - 1 + row_n - 1)

    def remote(src, dst, send, recv, device):
        return pltpu.make_async_remote_copy(
            src_ref=src, dst_ref=dst, send_sem=send, recv_sem=recv,
            device_id=device, device_id_type=MESH,
        )

    def col_slice(which):
        return pl.ds(pl.multiple_of(which * cols_t, cols_t), cols_t)

    def row_slice(which):
        return pl.ds(pl.multiple_of(which * rows_t, rows_t), rows_t)

    def send_a1(o, carry):
        to = lax.rem(c + o, key_n)
        remote(x_ref.at[pl.ds(to * per, per)], x1.at[:, col_slice(c)], a1_send.at[o], a1_recv.at[o], (r, to)).start()
        return carry

    def wait_a1(o, carry):
        to = lax.rem(c + key_n - o, key_n)
        copy = remote(x_ref.at[pl.ds(to * per, per)], x1.at[:, col_slice(to)], a1_send.at[o], a1_recv.at[o], (r, to))
        copy.wait_send()
        copy.wait_recv()
        return carry

    size = {"y": y_n, "z": z_n, "x": x_n}
    place = {"y": y, "z": z, "x": xx}

    def device(which_core, **at):
        at = {**place, **at}
        return (at["y"] * 2 + which_core, at["z"] * x_n + at["x"])

    def shifted(axis, d):
        return lax.rem(place[axis] + d, size[axis])

    class Gather:
        def __init__(self, buf, send, recv, axes):
            self.buf, self.send, self.recv = buf, send, recv
            self.first, self.others = axes[0], axes[1:]
            self.parts = size[axes[0]]
            self.turns = size[axes[1]] - 1

        def block(self, which_core, **at):
            at = {**place, **at}
            return self.buf.at[at["y"], which_core, at["z"], at["x"]]

        def copy(self, slot, ref, to):
            return remote(ref, ref, self.send.at[slot], self.recv.at[slot], to)

        def line(self, p, which_core, **at):
            u, v = self.others if p % 2 == 0 else self.others[::-1]
            return self.block(which_core, **{self.first: p, u: slice(None), v: at.get("v", place[v])})

        def one(self, d, out):
            near = shifted(self.first, size[self.first] - d)
            if out:
                return self.copy(d - 1, self.block(core), device(core, **{self.first: shifted(self.first, d)}))
            return self.copy(d - 1, self.block(core, **{self.first: near}), device(core, **{self.first: near}))

        def two(self, p, d, out):
            u = self.others[p % 2]
            slot = self.parts - 1 + p * self.turns + d - 1
            near = shifted(u, size[u] - d)
            if out:
                return self.copy(slot, self.block(core, **{self.first: p}), device(core, **{u: shifted(u, d)}))
            return self.copy(slot, self.block(core, **{self.first: p, u: near}), device(core, **{u: near}))

        def three(self, p, d, out):
            v = self.others[1 - p % 2]
            slot = self.parts - 1 + (self.parts + p) * self.turns + d - 1
            near = shifted(v, size[v] - d)
            if out:
                return self.copy(slot, self.line(p, core), device(core, **{v: shifted(v, d)}))
            return self.copy(slot, self.line(p, core, v=near), device(core, **{v: near}))

        def mate(self, p, d, out):
            v = self.others[1 - p % 2]
            slot = self.parts - 1 + 2 * self.parts * self.turns + p * (self.turns + 1) + d
            near = shifted(v, size[v] - d)
            return self.copy(slot, self.line(p, core if out else 1 - core, v=near), device(1 - core))

        def steps(self):
            return range(1, self.turns + 1)

        def start_one(self):
            for d in range(1, self.parts):
                self.one(d, True).start()

        def start_two(self):
            for d in range(1, self.parts):
                self.one(d, False).wait_recv()
            for p in range(self.parts):
                for d in self.steps():
                    self.two(p, d, True).start()

        def half(self, h):
            return range(h * self.parts // 2, (h + 1) * self.parts // 2)

        def start_three(self, h):
            for p in self.half(h):
                for d in self.steps():
                    self.two(p, d, False).wait_recv()
                for d in self.steps():
                    self.three(p, d, True).start()
                self.mate(p, 0, True).start()

        def pass_on(self, h):
            for d in self.steps():
                for p in self.half(h):
                    self.three(p, d, False).wait_recv()
                    self.mate(p, d, True).start()

        def finish(self, h):
            for p in self.half(h):
                for d in range(self.turns + 1):
                    self.mate(p, d, False).wait_recv()

        def drain(self):
            for d in range(1, self.parts):
                self.one(d, True).wait_send()
            for p in range(self.parts):
                for d in self.steps():
                    self.two(p, d, True).wait_send()
                    self.three(p, d, True).wait_send()
                for d in range(self.turns + 1):
                    self.mate(p, d, True).wait_send()

    lane_q = lax.broadcasted_iota(jnp.int32, (KEYS, LANES), 1)

    def prepare(m, xs, i):
        normed = layer_norm(xs[i].astype(F32), gain_ref[m : m + 1], shift_ref[m : m + 1]).astype(BF16)

        def project(part):
            return jnp.dot(normed, wp_ref[m, :, part * LANES : (part + 1) * LANES], preferred_element_type=F32)

        q_s[i] = (project(0) * HEAD**-0.5).astype(BF16)
        k = project(1).astype(BF16)
        v = project(2).astype(BF16)
        g_s[i] = jax.nn.sigmoid(project(3) + gb_ref[m : m + 1])
        for g in range(groups):
            kg = k[g * KEYS : (g + 1) * KEYS]
            vg = v[g * KEYS : (g + 1) * KEYS]
            for h in range(HEADS):
                mine = lane_q // HEAD == h
                at = g * LANES + h * KEYS
                k_s[i, at : at + KEYS, :] = jnp.where(mine, kg, jnp.zeros_like(kg))
                v_s[i, at : at + KEYS, :LANES] = jnp.where(mine, vg, jnp.zeros_like(vg))

    width = groups * LANES

    def score_chunk(row, at, s_s, n, top):
        s = lax.dot_general(
            q_s[row, at, :], k_s[row, n : n + CHUNK, :], (((1,), (1,)), ((), ())), preferred_element_type=F32
        )
        s = s + bias_s[at, n : n + CHUNK]
        s_s[:, n : n + CHUNK] = s
        for t in range(0, CHUNK, LANES):
            part = s[:, t : t + LANES]
            top = part if top is None else jnp.maximum(top, part)
        return top

    def weight_chunk(s_s, p_s, n, top):
        p_s[:, n : n + CHUNK] = jnp.exp2((s_s[:, n : n + CHUNK] - top) * LOG2E).astype(BF16)

    def attend(m, unit_done, between):
        units = 2 * per

        def where(unit):
            return lax.rem(unit, per), pl.ds(pl.multiple_of(unit // per * half_t, half_t), half_t)

        def scores(unit, s_s, slot, before=None):
            row, at = where(unit)
            top = None
            if before is not None:
                s_b, p_b, slot_b = before
                top_b = jnp.concatenate([top_s[slot_b]] * (CHUNK // LANES), axis=1)
            for n in range(0, width, CHUNK):
                if before is not None:
                    weight_chunk(s_b, p_b, n, top_b)
                top = score_chunk(row, at, s_s, n, top)
            top_s[slot] = head_max(top, lane)

        def weights(s_s, p_s, slot):
            top = jnp.concatenate([top_s[slot]] * (CHUNK // LANES), axis=1)
            for n in range(0, width, CHUNK):
                weight_chunk(s_s, p_s, n, top)

        def values(unit, p_s):
            row, at = where(unit)
            total = jnp.dot(p_s[...], v_s[row], preferred_element_type=F32)
            gated = (total[:, :LANES] / total[:, LANES:] * g_s[row, at, :]).astype(BF16)
            update = jnp.dot(gated, wo_ref[m], preferred_element_type=F32)
            unit_done(row, unit // per, at, update)

        scores(0, s_even, 0)

        def pair(t, carry):
            unit = 2 * t
            scores(unit + 1, s_odd, 1, (s_even, p_even, 0))
            values(unit, p_even)

            @pl.when(t == per // 2 - 1)
            def _():
                between()

            @pl.when(t < per - 1)
            def _():
                scores(unit + 2, s_even, 0, (s_odd, p_odd, 1))
                values(unit + 1, p_odd)

            @pl.when(t == per - 1)
            def _():
                weights(s_odd, p_odd, 1)
                values(unit + 1, p_odd)

            return carry

        lax.fori_loop(0, per, pair, 0)

    lax.fori_loop(1, key_n, send_a1, 0)
    x1[:, col_slice(c)] = x_ref[pl.ds(c * per, per)]

    tile_f[...] = layer_norm(x_ref[...].astype(F32), gain_ref[0:1], shift_ref[0:1])

    def pick(m, k):
        return jnp.where(lane_k % KEYS == k, wr_s[m], jnp.zeros((LANES, LANES), BF16))

    acc = jnp.zeros((rows_t, LANES), F32)
    for k in range(0, cols_t, 2):
        left = jnp.concatenate([tile_f[:, k, :], tile_f[:, k + 1, :]], axis=1).astype(BF16)
        right = jnp.concatenate([pick(0, k), pick(0, k + 1)], axis=0)
        acc = acc + jnp.dot(left, right, preferred_element_type=F32)
    bias_a[y, core, z, xx] = acc.astype(BF16)

    def more(m, xs, lo, hi):
        def one(i, carry):
            prepare(m, xs, i)
            return carry

        lax.fori_loop(lo, hi, one, 0)

    def widen_one(h):
        def widen(g, carry):
            at = pl.ds(pl.multiple_of(g * LANES, LANES), LANES)
            masked = key_bias(g)
            for rr in range(h * row_n // 2, (h + 1) * row_n // 2):
                block = bias_a[rr // 2, rr % 2, g // x_n, lax.rem(g, x_n)].astype(F32)
                bias_s[rr * rows_t : (rr + 1) * rows_t, at] = block + masked
            return carry

        lax.fori_loop(0, key_n, widen, 0)

    moves = Gather(bias_a, ga_send, ga_recv, "yzx")
    moves.start_one()
    moves.start_two()
    lax.fori_loop(1, key_n, wait_a1, 0)
    more(0, x1, 0, 1)
    moves.start_three(0)
    moves.start_three(1)
    more(0, x1, 1, per)
    moves.pass_on(0)
    moves.finish(0)
    widen_one(0)

    def a2_copy(i, n, to, frm):
        return remote(
            as1.at[pl.ds(i, n), col_slice(to)], t2.at[pl.ds(frm * per + i, n)], a2_send.at[to], a2_recv.at[frm], (r, to)
        )

    def unit_one(i, h, at, update):
        keep = kept(h * half_t, rows_t * r + per * c + i, half_t)
        as1[i, at, :] = (x1[i, at, :].astype(F32) + keep * update).astype(BF16)

        def send(o, inner):
            to = h * (key_n // 2) + lax.rem(c + o, key_n // 2)

            @pl.when(to != c)
            def _():
                a2_copy(i, 1, to, c).start()

            return inner

        lax.fori_loop(0, key_n // 2, send, 0)

    def between_one():
        moves.pass_on(1)
        moves.finish(1)
        widen_one(1)

    attend(0, unit_one, between_one)
    t2[pl.ds(per * c, per)] = as1[:, col_slice(c)]
    moves.drain()

    def wait_a2(o, carry):
        to = lax.rem(c + o, key_n)
        a2_copy(0, per, to, c).wait_send()
        frm = lax.rem(c + key_n - o, key_n)
        copy = remote(
            as1.at[pl.ds(0, per), col_slice(c)], t2.at[pl.ds(frm * per, per)], a2_send.at[frm], a2_recv.at[frm], (r, frm)
        )
        copy.wait_recv()
        return carry

    lax.fori_loop(1, key_n, wait_a2, 0)

    tile_f[...] = t2[...].astype(F32)
    for j in range(cols_t):
        sb[j] = tile_f[:, j, :].astype(BF16)

    def b2_copy(o, to, frm):
        return remote(sb.at[pl.ds(to * per, per)], x2.at[:, row_slice(frm)], b2_send.at[o], b2_recv.at[o], (to, c))

    def send_b2(o, carry):
        b2_copy(o, lax.rem(r + o, row_n), r).start()
        return carry

    def wait_b2(o, carry):
        b2_copy(o, lax.rem(r + o, row_n), r).wait_send()
        frm = lax.rem(r + row_n - o, row_n)
        b2_copy(o, frm, frm).wait_recv()
        return carry

    tile_f[...] = layer_norm(tile_f[...], gain_ref[1:2], shift_ref[1:2])
    halves = rows_t // KEYS

    acc = jnp.zeros((rows_t, LANES), F32)
    for k in range(0, KEYS, 2):
        left = jnp.concatenate(
            [jnp.concatenate([tile_f[h * KEYS + kk] for h in range(halves)], axis=0) for kk in (k, k + 1)], axis=1
        ).astype(BF16)
        right = jnp.concatenate([pick(1, k), pick(1, k + 1)], axis=0)
        acc = acc + jnp.dot(left, right, preferred_element_type=F32)
    bias_b[y, core, z, xx] = acc.astype(BF16)

    moves_two = Gather(bias_b, gb_send, gb_recv, "zyx")
    moves_two.start_one()
    lax.fori_loop(1, row_n, send_b2, 0)
    x2[:, row_slice(r)] = sb[pl.ds(r * per, per)]
    moves_two.start_two()
    lax.fori_loop(1, row_n, wait_b2, 0)
    more(1, x2, 0, 1)
    moves_two.start_three(0)
    moves_two.start_three(1)
    more(1, x2, 1, per)
    moves_two.pass_on(0)
    moves_two.finish(0)

    def widen_two(h):
        def widen(g, carry):
            for gg in range(row_n * halves):
                rr, hh = gg // halves, gg % halves
                block = bias_b[rr // 2, rr % 2, g // x_n, lax.rem(g, x_n), hh * KEYS : (hh + 1) * KEYS, :].astype(F32)
                bias_s[col_slice(g), gg * LANES : (gg + 1) * LANES] = block + key_bias(gg)
            return carry

        lax.fori_loop(h * key_n // 2, (h + 1) * key_n // 2, widen, 0)

    widen_two(0)

    def c2_copy(i, n, to, frm):
        return remote(
            np2.at[pl.ds(i, n), row_slice(to)], fin.at[pl.ds(frm * per + i, n)], c2_send.at[to], c2_recv.at[frm], (to, c)
        )

    def unit_two(i, h, at, update):
        keep = kept(h * half_t, cols_t * c + per * r + i, half_t)
        update = (keep * update).astype(BF16).astype(F32)
        np2[i, at, :] = (x2[i, at, :].astype(F32) + update).astype(BF16)

        def send(o, inner):
            to = h * (row_n // 2) + lax.rem(r + o, row_n // 2)

            @pl.when(to != r)
            def _():
                c2_copy(i, 1, to, r).start()

            return inner

        lax.fori_loop(0, row_n // 2, send, 0)

    def between_two():
        moves_two.pass_on(1)
        moves_two.finish(1)
        widen_two(1)

    attend(1, unit_two, between_two)
    fin[pl.ds(per * r, per)] = np2[:, row_slice(r)]
    moves_two.drain()

    def wait_c2(o, carry):
        c2_copy(0, per, lax.rem(r + o, row_n), r).wait_send()
        frm = lax.rem(r + row_n - o, row_n)
        copy = remote(
            np2.at[pl.ds(0, per), row_slice(r)], fin.at[pl.ds(frm * per, per)], c2_send.at[frm], c2_recv.at[frm], (frm, c)
        )
        copy.wait_recv()
        return carry

    lax.fori_loop(1, row_n, wait_c2, 0)


def local(row_n, key_n, pair_rep, token_mask, norm_gain, norm_shift, w_proj, w_bias, gate_bias, w_out):
    rows_t, cols_t, channels = pair_rep.shape
    tokens = token_mask.shape[0]
    per = tokens // (row_n * key_n)
    groups = tokens // KEYS
    width = groups * LANES
    y_n, z_n = row_n // 2, int(round(key_n**0.5))
    slots = y_n - 1 + 2 * y_n * (z_n - 1) + y_n * z_n
    vmem, dma = pltpu.VMEM, pltpu.SemaphoreType.DMA
    buf = (y_n, 2, z_n, z_n, rows_t, LANES)
    turned = pl.pallas_call(
        functools.partial(kernel, tokens, row_n, key_n),
        out_shape=jax.ShapeDtypeStruct((cols_t, rows_t, channels), BF16),
        in_specs=[pl.BlockSpec(memory_space=pl.ANY)] + [pl.BlockSpec(memory_space=pltpu.VMEM)] * 7,
        out_specs=pl.BlockSpec(memory_space=pltpu.VMEM),
        scratch_shapes=[
            vmem((per, tokens, LANES), BF16),
            vmem((per, tokens, LANES), BF16),
            vmem((per, tokens, LANES), BF16),
            vmem((per, tokens, LANES), BF16),
            vmem((rows_t, cols_t, LANES), BF16),
            vmem((cols_t, rows_t, LANES), BF16),
            vmem((rows_t, cols_t, LANES), F32),
            vmem(buf, BF16),
            vmem(buf, BF16),
            vmem((tokens, width), F32),
            vmem((per, tokens, LANES), BF16),
            vmem((per, width, LANES), BF16),
            vmem((per, width, 2 * LANES), BF16),
            vmem((per, tokens, LANES), F32),
            vmem((tokens // 2, width), F32),
            vmem((tokens // 2, width), F32),
            vmem((tokens // 2, width), BF16),
            vmem((tokens // 2, width), BF16),
            vmem((2, tokens // 2, LANES), F32),
            vmem((2, LANES, LANES), BF16),
            vmem((rows_t, cols_t, LANES), BF16),
            dma,
            dma((key_n,)), dma((key_n,)), dma((key_n,)), dma((key_n,)),
            dma((row_n,)), dma((row_n,)), dma((row_n,)), dma((row_n,)),
            dma((slots,)), dma((slots,)), dma((slots,)), dma((slots,)),
        ],
        compiler_params=pltpu.CompilerParams(
            collective_id=0, has_side_effects=True, vmem_limit_bytes=56 * 2**20
        ),
        name="triangle_attention",
    )(
        pair_rep, token_mask.reshape(-1, min(tokens, LANES)), norm_gain, norm_shift, w_proj, w_bias.transpose(0, 2, 1), gate_bias,
        w_out,
    )
    return turned.transpose(1, 0, 2)


def solution(mesh):
    row_n, key_n = mesh.shape["rows"], mesh.shape["keys"]
    in_specs = (P("rows", "keys", None), P(), P(), P(), P(), P(), P(), P())
    out_specs = P("rows", "keys", None)
    return jax.shard_map(
        functools.partial(local, row_n, key_n), mesh=mesh, in_specs=in_specs, out_specs=out_specs, check_vma=False
    )
```

```python
import functools

import jax
import jax.numpy as jnp
from jax import lax
from jax.experimental import pallas as pl
from jax.experimental.pallas import tpu as pltpu
from jax.sharding import PartitionSpec as P

MESH = pl.DeviceIdType.MESH
LOG2E = 1.4426950408889634
F32 = jnp.float32
BF16 = jnp.bfloat16
KEYS = 32
HEADS = 4
HEAD = 32
LANES = 128
CHUNK = 256


def layer_norm(values, gain, shift):
    center = jnp.mean(values, axis=-1, keepdims=True)
    moved = values - center
    spread = jnp.mean(moved * moved, axis=-1, keepdims=True)
    return moved * lax.rsqrt(spread + 1e-05) * gain + shift


def head_max(m, lane):
    for step in (16, 8, 4, 2, 1):
        below = pltpu.roll(m, step, 1)
        above = pltpu.roll(m, LANES - step, 1)
        m = jnp.maximum(m, jnp.where((lane & step) != 0, below, above))
    return m


def kernel(
    tokens, row_n, key_n,
    x_hbm, mask_ref, gain_ref, shift_ref, wp_ref, wb_ref, gb_ref, wo_ref,
    fin,
    x1, x2, as1, np2, t2, sb, tile_f, bias_a, bias_b, bias_s, q_s, k_s, v_s, g_s,
    s_even, s_odd, p_even, p_odd, top_s, wr_s, x_ref, x_sem,
    a1_send, a1_recv, a2_send, a2_recv, b2_send, b2_recv, c2_send, c2_recv,
    ga_send, ga_recv, gb_send, gb_recv,
):
    rows_t, cols_t = tokens // row_n, tokens // key_n
    per = tokens // (row_n * key_n)
    groups = tokens // KEYS
    y_n = row_n // 2
    z_n = x_n = int(round(key_n**0.5))
    half_t = tokens // 2
    r, c = lax.axis_index("rows"), lax.axis_index("keys")
    y, core = r // 2, r % 2
    z, xx = c // x_n, c % x_n
    lane = lax.broadcasted_iota(jnp.int32, (1, LANES), 1)

    barrier = pltpu.get_barrier_semaphore()
    x_copy = pltpu.make_async_copy(x_hbm, x_ref, x_sem)
    x_copy.start()

    def greet_keys(o, carry):
        pl.semaphore_signal(barrier, inc=1, device_id=(r, lax.rem(c + o, key_n)), device_id_type=MESH)
        return carry

    def greet_rows(o, carry):
        pl.semaphore_signal(barrier, inc=1, device_id=(lax.rem(r + o, row_n), c), device_id_type=MESH)
        return carry

    lax.fori_loop(1, key_n, greet_keys, 0)
    lax.fori_loop(1, row_n, greet_rows, 0)

    real = jnp.sum(mask_ref[...], keepdims=True)

    def key_bias(g):
        key = g * KEYS + lane % KEYS
        return jnp.where(key < real, 0.0, -1000000000.0)

    def kept(first, token, count):
        at = first + lax.broadcasted_iota(jnp.int32, (count, LANES), 0)
        return jnp.where(jnp.logical_and(at < real, token < real), 1.0, 0.0)

    lane_k = lax.broadcasted_iota(jnp.int32, (LANES, LANES), 1)
    sub_k = lax.broadcasted_iota(jnp.int32, (LANES, LANES), 0)
    ones = jnp.where(lane_k // HEAD == sub_k // KEYS, 1.0, 0.0).astype(BF16)

    def put_ones(i, carry):
        for g in range(groups):
            v_s[i, g * LANES : (g + 1) * LANES, LANES:] = ones
        return carry

    lax.fori_loop(0, per, put_ones, 0)
    spread = lax.broadcasted_iota(jnp.int32, (HEADS, LANES), 0) == lax.broadcasted_iota(jnp.int32, (HEADS, LANES), 1) // KEYS
    spread = jnp.where(spread, 1.0, 0.0).astype(BF16)
    for m in range(2):
        wr_s[m] = lax.dot_general(
            wb_ref[m], spread, (((0,), (0,)), ((), ())), preferred_element_type=F32
        ).astype(BF16)
    x_copy.wait()
    pl.semaphore_wait(barrier, key_n - 1 + row_n - 1)

    def remote(src, dst, send, recv, device):
        return pltpu.make_async_remote_copy(
            src_ref=src, dst_ref=dst, send_sem=send, recv_sem=recv,
            device_id=device, device_id_type=MESH,
        )

    def col_slice(which):
        return pl.ds(pl.multiple_of(which * cols_t, cols_t), cols_t)

    def row_slice(which):
        return pl.ds(pl.multiple_of(which * rows_t, rows_t), rows_t)

    def send_a1(o, carry):
        to = lax.rem(c + o, key_n)
        remote(x_ref.at[pl.ds(to * per, per)], x1.at[:, col_slice(c)], a1_send.at[o], a1_recv.at[o], (r, to)).start()
        return carry

    def wait_a1(o, carry):
        to = lax.rem(c + key_n - o, key_n)
        copy = remote(x_ref.at[pl.ds(to * per, per)], x1.at[:, col_slice(to)], a1_send.at[o], a1_recv.at[o], (r, to))
        copy.wait_send()
        copy.wait_recv()
        return carry

    size = {"y": y_n, "z": z_n, "x": x_n}
    place = {"y": y, "z": z, "x": xx}

    def device(which_core, **at):
        at = {**place, **at}
        return (at["y"] * 2 + which_core, at["z"] * x_n + at["x"])

    def shifted(axis, d):
        return lax.rem(place[axis] + d, size[axis])

    class Gather:
        def __init__(self, buf, send, recv, axes):
            self.buf, self.send, self.recv = buf, send, recv
            self.first, self.others = axes[0], axes[1:]
            self.parts = size[axes[0]]
            self.turns = size[axes[1]] - 1

        def block(self, which_core, **at):
            at = {**place, **at}
            return self.buf.at[at["y"], which_core, at["z"], at["x"]]

        def copy(self, slot, ref, to):
            return remote(ref, ref, self.send.at[slot], self.recv.at[slot], to)

        def line(self, p, which_core, **at):
            u, v = self.others if p % 2 == 0 else self.others[::-1]
            return self.block(which_core, **{self.first: p, u: slice(None), v: at.get("v", place[v])})

        def one(self, d, out):
            near = shifted(self.first, size[self.first] - d)
            if out:
                return self.copy(d - 1, self.block(core), device(core, **{self.first: shifted(self.first, d)}))
            return self.copy(d - 1, self.block(core, **{self.first: near}), device(core, **{self.first: near}))

        def two(self, p, d, out):
            u = self.others[p % 2]
            slot = self.parts - 1 + p * self.turns + d - 1
            near = shifted(u, size[u] - d)
            if out:
                return self.copy(slot, self.block(core, **{self.first: p}), device(core, **{u: shifted(u, d)}))
            return self.copy(slot, self.block(core, **{self.first: p, u: near}), device(core, **{u: near}))

        def three(self, p, d, out):
            v = self.others[1 - p % 2]
            slot = self.parts - 1 + (self.parts + p) * self.turns + d - 1
            near = shifted(v, size[v] - d)
            if out:
                return self.copy(slot, self.line(p, core), device(core, **{v: shifted(v, d)}))
            return self.copy(slot, self.line(p, core, v=near), device(core, **{v: near}))

        def mate(self, p, d, out):
            v = self.others[1 - p % 2]
            slot = self.parts - 1 + 2 * self.parts * self.turns + p * (self.turns + 1) + d
            near = shifted(v, size[v] - d)
            return self.copy(slot, self.line(p, core if out else 1 - core, v=near), device(1 - core))

        def steps(self):
            return range(1, self.turns + 1)

        def start_one(self):
            for d in range(1, self.parts):
                self.one(d, True).start()

        def start_two(self, h):
            for d in range(1, self.parts):
                near = shifted(self.first, self.parts - d)

                @pl.when(near // (self.parts // 2) == h)
                def _(d=d):
                    self.one(d, False).wait_recv()

            for p in self.half(h):
                for d in self.steps():
                    self.two(p, d, True).start()

        def half(self, h):
            return range(h * self.parts // 2, (h + 1) * self.parts // 2)

        def start_three(self, h):
            for p in self.half(h):
                for d in self.steps():
                    self.two(p, d, False).wait_recv()
                for d in self.steps():
                    self.three(p, d, True).start()
                self.mate(p, 0, True).start()

        def pass_on(self, h):
            for d in self.steps():
                for p in self.half(h):
                    self.three(p, d, False).wait_recv()
                    self.mate(p, d, True).start()

        def finish(self, h):
            for p in self.half(h):
                for d in range(self.turns + 1):
                    self.mate(p, d, False).wait_recv()

        def drain(self):
            for d in range(1, self.parts):
                self.one(d, True).wait_send()
            for p in range(self.parts):
                for d in self.steps():
                    self.two(p, d, True).wait_send()
                    self.three(p, d, True).wait_send()
                for d in range(self.turns + 1):
                    self.mate(p, d, True).wait_send()

    lane_q = lax.broadcasted_iota(jnp.int32, (KEYS, LANES), 1)

    def prepare(m, xs, i):
        normed = layer_norm(xs[i].astype(F32), gain_ref[m : m + 1], shift_ref[m : m + 1]).astype(BF16)

        def project(part):
            return jnp.dot(normed, wp_ref[m, :, part * LANES : (part + 1) * LANES], preferred_element_type=F32)

        q_s[i] = (project(0) * HEAD**-0.5).astype(BF16)
        k = project(1).astype(BF16)
        v = project(2).astype(BF16)
        g_s[i] = jax.nn.sigmoid(project(3) + gb_ref[m : m + 1])
        for g in range(groups):
            kg = k[g * KEYS : (g + 1) * KEYS]
            vg = v[g * KEYS : (g + 1) * KEYS]
            for h in range(HEADS):
                mine = lane_q // HEAD == h
                at = g * LANES + h * KEYS
                k_s[i, at : at + KEYS, :] = jnp.where(mine, kg, jnp.zeros_like(kg))
                v_s[i, at : at + KEYS, :LANES] = jnp.where(mine, vg, jnp.zeros_like(vg))

    width = groups * LANES

    def score_chunk(row, at, s_s, n, top):
        s = lax.dot_general(
            q_s[row, at, :], k_s[row, n : n + CHUNK, :], (((1,), (1,)), ((), ())), preferred_element_type=F32
        )
        s = s + bias_s[at, n : n + CHUNK]
        s_s[:, n : n + CHUNK] = s
        for t in range(0, CHUNK, LANES):
            part = s[:, t : t + LANES]
            top = part if top is None else jnp.maximum(top, part)
        return top

    def weight_chunk(s_s, p_s, n, top):
        p_s[:, n : n + CHUNK] = jnp.exp2((s_s[:, n : n + CHUNK] - top) * LOG2E).astype(BF16)

    def attend(m, unit_done, hooks):
        units = 2 * per

        def where(unit):
            return lax.rem(unit, per), pl.ds(pl.multiple_of(unit // per * half_t, half_t), half_t)

        def scores(unit, s_s, slot, before=None):
            row, at = where(unit)
            top = None
            if before is not None:
                s_b, p_b, slot_b = before
                top_b = jnp.concatenate([top_s[slot_b]] * (CHUNK // LANES), axis=1)
            for n in range(0, width, CHUNK):
                if before is not None:
                    weight_chunk(s_b, p_b, n, top_b)
                top = score_chunk(row, at, s_s, n, top)
            top_s[slot] = head_max(top, lane)

        def weights(s_s, p_s, slot):
            top = jnp.concatenate([top_s[slot]] * (CHUNK // LANES), axis=1)
            for n in range(0, width, CHUNK):
                weight_chunk(s_s, p_s, n, top)

        def values(unit, p_s):
            row, at = where(unit)
            total = jnp.dot(p_s[...], v_s[row], preferred_element_type=F32)
            gated = (total[:, :LANES] / total[:, LANES:] * g_s[row, at, :]).astype(BF16)
            update = jnp.dot(gated, wo_ref[m], preferred_element_type=F32)
            unit_done(row, unit // per, at, update)

        scores(0, s_even, 0)

        def pair(t, carry):
            unit = 2 * t

            def run_hooks(odd):
                for after, hook in hooks.items():
                    if after % 2 == odd:
                        pl.when(t == after // 2)(hook)

            scores(unit + 1, s_odd, 1, (s_even, p_even, 0))
            values(unit, p_even)
            run_hooks(0)

            @pl.when(t < per - 1)
            def _():
                scores(unit + 2, s_even, 0, (s_odd, p_odd, 1))
                values(unit + 1, p_odd)

            @pl.when(t == per - 1)
            def _():
                weights(s_odd, p_odd, 1)
                values(unit + 1, p_odd)

            run_hooks(1)
            return carry

        lax.fori_loop(0, per, pair, 0)

    lax.fori_loop(1, key_n, send_a1, 0)
    x1[:, col_slice(c)] = x_ref[pl.ds(c * per, per)]

    tile_f[...] = layer_norm(x_ref[...].astype(F32), gain_ref[0:1], shift_ref[0:1])

    def pick(m, k):
        return jnp.where(lane_k % KEYS == k, wr_s[m], jnp.zeros((LANES, LANES), BF16))

    acc = jnp.zeros((rows_t, LANES), F32)
    for k in range(0, cols_t, 2):
        left = jnp.concatenate([tile_f[:, k, :], tile_f[:, k + 1, :]], axis=1).astype(BF16)
        right = jnp.concatenate([pick(0, k), pick(0, k + 1)], axis=0)
        acc = acc + jnp.dot(left, right, preferred_element_type=F32)
    bias_a[y, core, z, xx] = acc.astype(BF16)

    def more(m, xs, lo, hi):
        def one(i, carry):
            prepare(m, xs, i)
            return carry

        lax.fori_loop(lo, hi, one, 0)

    def widen_one(h):
        def widen(g, carry):
            at = pl.ds(pl.multiple_of(g * LANES, LANES), LANES)
            masked = key_bias(g)
            for rr in range(h * row_n // 2, (h + 1) * row_n // 2):
                block = bias_a[rr // 2, rr % 2, g // x_n, lax.rem(g, x_n)].astype(F32)
                bias_s[rr * rows_t : (rr + 1) * rows_t, at] = block + masked
            return carry

        lax.fori_loop(0, key_n, widen, 0)

    moves = Gather(bias_a, ga_send, ga_recv, "yzx")
    moves.start_one()
    moves.start_two(0)
    lax.fori_loop(1, key_n, wait_a1, 0)
    more(0, x1, 0, 1)
    moves.start_three(0)
    moves.start_two(1)
    more(0, x1, 1, per)
    moves.pass_on(0)
    moves.start_three(1)
    moves.finish(0)
    widen_one(0)

    def a2_copy(i, n, to, frm):
        return remote(
            as1.at[pl.ds(i, n), col_slice(to)], t2.at[pl.ds(frm * per + i, n)], a2_send.at[to], a2_recv.at[frm], (r, to)
        )

    def unit_one(i, h, at, update):
        keep = kept(h * half_t, rows_t * r + per * c + i, half_t)
        as1[i, at, :] = (x1[i, at, :].astype(F32) + keep * update).astype(BF16)

        def send(o, inner):
            to = h * (key_n // 2) + lax.rem(c + o, key_n // 2)

            @pl.when(to != c)
            def _():
                a2_copy(i, 1, to, c).start()

            return inner

        lax.fori_loop(0, key_n // 2, send, 0)

    def between_one():
        moves.finish(1)
        widen_one(1)

    def sent_a2(o, carry):
        a2_copy(0, per, lax.rem(c + o, key_n), c).wait_send()
        return carry

    def wait_a2(o, carry):
        frm = lax.rem(c + key_n - o, key_n)
        copy = remote(
            as1.at[pl.ds(0, per), col_slice(c)], t2.at[pl.ds(frm * per, per)], a2_send.at[frm], a2_recv.at[frm], (r, frm)
        )
        copy.wait_recv()
        return carry

    moves_two = Gather(bias_b, gb_send, gb_recv, "zyx")
    halves = rows_t // KEYS

    def b2_row(a, o, to):
        return remote(sb.at[to * per + a], x2.at[a, row_slice(r)], b2_send.at[o], b2_recv.at[a], (to, c))

    def b2_own(a):
        return pltpu.make_async_copy(sb.at[r * per + a], x2.at[a, row_slice(r)], b2_recv.at[a])

    def send_b2(a, carry):
        def send(o, inner):
            b2_row(a, o, lax.rem(r + o, row_n)).start()
            return inner

        lax.fori_loop(1, row_n, send, 0)
        b2_own(a).start()
        return carry

    def wait_b2(a):
        pltpu.make_async_copy(x2.at[a], x2.at[a], b2_recv.at[a]).wait()

    def sent_b2(o, carry):
        to = lax.rem(r + o, row_n)
        rows_out = sb.at[pl.ds(to * per, per)]
        remote(rows_out, rows_out, b2_send.at[o], b2_recv.at[0], (to, c)).wait_send()
        return carry

    def second_tile():
        lax.fori_loop(1, key_n, wait_a2, 0)
        t2[pl.ds(per * c, per)] = as1[:, col_slice(c)]
        tile_f[...] = t2[...].astype(F32)
        for j in range(cols_t):
            sb[j] = tile_f[:, j, :].astype(BF16)
        lax.fori_loop(0, per, send_b2, 0)
        tile_f[...] = layer_norm(tile_f[...], gain_ref[1:2], shift_ref[1:2])
        acc = jnp.zeros((rows_t, LANES), F32)
        for k in range(0, KEYS, 2):
            left = jnp.concatenate(
                [jnp.concatenate([tile_f[h * KEYS + kk] for h in range(halves)], axis=0) for kk in (k, k + 1)], axis=1
            ).astype(BF16)
            right = jnp.concatenate([pick(1, k), pick(1, k + 1)], axis=0)
            acc = acc + jnp.dot(left, right, preferred_element_type=F32)
        bias_b[y, core, z, xx] = acc.astype(BF16)
        moves_two.start_one()

    early = z < z_n // 2

    def early_tile():
        pl.when(early)(second_tile)

    attend(0, unit_one, {per - 3: lambda: moves.pass_on(1), per - 2: between_one, per + 1: early_tile})
    moves_two.start_two(0)
    pl.when(jnp.logical_not(early))(second_tile)
    moves_two.start_three(0)
    wait_b2(0)
    prepare(1, x2, 0)
    moves_two.start_two(1)

    def late_row(a, carry):
        wait_b2(a)
        prepare(1, x2, a)
        return carry

    lax.fori_loop(1, per, late_row, 0)
    moves_two.pass_on(0)
    moves_two.start_three(1)
    moves_two.finish(0)

    def widen_two(h):
        def widen(g, carry):
            for gg in range(row_n * halves):
                rr, hh = gg // halves, gg % halves
                block = bias_b[rr // 2, rr % 2, g // x_n, lax.rem(g, x_n), hh * KEYS : (hh + 1) * KEYS, :].astype(F32)
                bias_s[col_slice(g), gg * LANES : (gg + 1) * LANES] = block + key_bias(gg)
            return carry

        lax.fori_loop(h * key_n // 2, (h + 1) * key_n // 2, widen, 0)

    widen_two(0)

    def c2_copy(i, n, to, frm):
        return remote(
            np2.at[pl.ds(i, n), row_slice(to)], fin.at[pl.ds(frm * per + i, n)], c2_send.at[to], c2_recv.at[frm], (to, c)
        )

    def unit_two(i, h, at, update):
        keep = kept(h * half_t, cols_t * c + per * r + i, half_t)
        update = (keep * update).astype(BF16).astype(F32)
        np2[i, at, :] = (x2[i, at, :].astype(F32) + update).astype(BF16)

        def send(o, inner):
            to = h * (row_n // 2) + lax.rem(r + o, row_n // 2)

            @pl.when(to != r)
            def _():
                c2_copy(i, 1, to, r).start()

            return inner

        lax.fori_loop(0, row_n // 2, send, 0)

    def between_two():
        moves_two.finish(1)
        widen_two(1)

    attend(1, unit_two, {per - 3: lambda: moves_two.pass_on(1), per - 2: between_two})
    fin[pl.ds(per * r, per)] = np2[:, row_slice(r)]
    moves.drain()
    moves_two.drain()
    lax.fori_loop(1, key_n, sent_a2, 0)
    lax.fori_loop(1, row_n, sent_b2, 0)

    def wait_c2(o, carry):
        c2_copy(0, per, lax.rem(r + o, row_n), r).wait_send()
        frm = lax.rem(r + row_n - o, row_n)
        copy = remote(
            np2.at[pl.ds(0, per), row_slice(r)], fin.at[pl.ds(frm * per, per)], c2_send.at[frm], c2_recv.at[frm], (frm, c)
        )
        copy.wait_recv()
        return carry

    lax.fori_loop(1, row_n, wait_c2, 0)


def local(row_n, key_n, pair_rep, token_mask, norm_gain, norm_shift, w_proj, w_bias, gate_bias, w_out):
    rows_t, cols_t, channels = pair_rep.shape
    tokens = token_mask.shape[0]
    per = tokens // (row_n * key_n)
    groups = tokens // KEYS
    width = groups * LANES
    y_n, z_n = row_n // 2, int(round(key_n**0.5))
    slots = y_n - 1 + 2 * y_n * (z_n - 1) + y_n * z_n
    vmem, dma = pltpu.VMEM, pltpu.SemaphoreType.DMA
    buf = (y_n, 2, z_n, z_n, rows_t, LANES)
    turned = pl.pallas_call(
        functools.partial(kernel, tokens, row_n, key_n),
        out_shape=jax.ShapeDtypeStruct((cols_t, rows_t, channels), BF16),
        in_specs=[pl.BlockSpec(memory_space=pl.ANY)] + [pl.BlockSpec(memory_space=pltpu.VMEM)] * 7,
        out_specs=pl.BlockSpec(memory_space=pltpu.VMEM),
        scratch_shapes=[
            vmem((per, tokens, LANES), BF16),
            vmem((per, tokens, LANES), BF16),
            vmem((per, tokens, LANES), BF16),
            vmem((per, tokens, LANES), BF16),
            vmem((rows_t, cols_t, LANES), BF16),
            vmem((cols_t, rows_t, LANES), BF16),
            vmem((rows_t, cols_t, LANES), F32),
            vmem(buf, BF16),
            vmem(buf, BF16),
            vmem((tokens, width), F32),
            vmem((per, tokens, LANES), BF16),
            vmem((per, width, LANES), BF16),
            vmem((per, width, 2 * LANES), BF16),
            vmem((per, tokens, LANES), F32),
            vmem((tokens // 2, width), F32),
            vmem((tokens // 2, width), F32),
            vmem((tokens // 2, width), BF16),
            vmem((tokens // 2, width), BF16),
            vmem((2, tokens // 2, LANES), F32),
            vmem((2, LANES, LANES), BF16),
            vmem((rows_t, cols_t, LANES), BF16),
            dma,
            dma((key_n,)), dma((key_n,)), dma((key_n,)), dma((key_n,)),
            dma((row_n,)), dma((row_n,)), dma((row_n,)), dma((row_n,)),
            dma((slots,)), dma((slots,)), dma((slots,)), dma((slots,)),
        ],
        compiler_params=pltpu.CompilerParams(
            collective_id=0, has_side_effects=True, vmem_limit_bytes=56 * 2**20
        ),
        name="triangle_attention",
    )(
        pair_rep, token_mask.reshape(-1, min(tokens, LANES)), norm_gain, norm_shift, w_proj, w_bias.transpose(0, 2, 1), gate_bias,
        w_out,
    )
    return turned.transpose(1, 0, 2)


def solution(mesh):
    row_n, key_n = mesh.shape["rows"], mesh.shape["keys"]
    in_specs = (P("rows", "keys", None), P(), P(), P(), P(), P(), P(), P())
    out_specs = P("rows", "keys", None)
    return jax.shard_map(
        functools.partial(local, row_n, key_n), mesh=mesh, in_specs=in_specs, out_specs=out_specs, check_vma=False
    )
```

```python
import functools

import jax
import jax.numpy as jnp
from jax import lax
from jax.experimental import pallas as pl
from jax.experimental.pallas import tpu as pltpu
from jax.sharding import PartitionSpec as P

MESH = pl.DeviceIdType.MESH
LOG2E = 1.4426950408889634
F32 = jnp.float32
BF16 = jnp.bfloat16
KEYS = 32
HEADS = 4
HEAD = 32
LANES = 128
CHUNK = 256


def layer_norm(values, gain, shift):
    center = jnp.mean(values, axis=-1, keepdims=True)
    moved = values - center
    spread = jnp.mean(moved * moved, axis=-1, keepdims=True)
    return moved * lax.rsqrt(spread + 1e-05) * gain + shift


def head_max(m, lane):
    for step in (16, 8, 4, 2, 1):
        below = pltpu.roll(m, step, 1)
        above = pltpu.roll(m, LANES - step, 1)
        m = jnp.maximum(m, jnp.where((lane & step) != 0, below, above))
    return m


def kernel(
    tokens, row_n, key_n,
    x_hbm, mask_ref, gain_ref, shift_ref, wp_hbm, wb_ref, gb_ref, wo_hbm,
    fin,
    x1, x2, as1, np2, t2, sb, tile_f, bias_a, bias_b, bias_s, q_s, k_s, v_s, g_s,
    s_even, s_odd, p_even, p_odd, top_s, wr_s, x_ref, wp_ref, wo_ref, x_sem,
    a1_send, a1_recv, a2_send, a2_recv, b2_send, b2_recv, c2_send, c2_recv,
    ga_send, ga_recv, gb_send, gb_recv,
):
    rows_t, cols_t = tokens // row_n, tokens // key_n
    per = tokens // (row_n * key_n)
    groups = tokens // KEYS
    y_n = row_n // 2
    z_n = x_n = int(round(key_n**0.5))
    half_t = tokens // 2
    r, c = lax.axis_index("rows"), lax.axis_index("keys")
    y, core = r // 2, r % 2
    z, xx = c // x_n, c % x_n
    lane = lax.broadcasted_iota(jnp.int32, (1, LANES), 1)

    barrier = pltpu.get_barrier_semaphore()
    x_copy = pltpu.make_async_copy(x_hbm, x_ref, x_sem.at[0])
    x_copy.start()
    w_copies = (
        pltpu.make_async_copy(wp_hbm, wp_ref, x_sem.at[1]),
        pltpu.make_async_copy(wo_hbm, wo_ref, x_sem.at[2]),
    )
    for copy in w_copies:
        copy.start()

    def greet_keys(o, carry):
        pl.semaphore_signal(barrier, inc=1, device_id=(r, lax.rem(c + o, key_n)), device_id_type=MESH)
        return carry

    def greet_rows(o, carry):
        pl.semaphore_signal(barrier, inc=1, device_id=(lax.rem(r + o, row_n), c), device_id_type=MESH)
        return carry

    lax.fori_loop(1, key_n, greet_keys, 0)
    lax.fori_loop(1, row_n, greet_rows, 0)

    real = jnp.sum(mask_ref[...], keepdims=True)

    def key_bias(g):
        key = g * KEYS + lane % KEYS
        return jnp.where(key < real, 0.0, -1000000000.0)

    def kept(first, token, count):
        at = first + lax.broadcasted_iota(jnp.int32, (count, LANES), 0)
        return jnp.where(jnp.logical_and(at < real, token < real), 1.0, 0.0)

    lane_k = lax.broadcasted_iota(jnp.int32, (LANES, LANES), 1)
    sub_k = lax.broadcasted_iota(jnp.int32, (LANES, LANES), 0)
    ones = jnp.where(lane_k // HEAD == sub_k // KEYS, 1.0, 0.0).astype(BF16)

    def put_ones(i, carry):
        for g in range(groups):
            v_s[i, g * LANES : (g + 1) * LANES, LANES:] = ones
        return carry

    spread = lax.broadcasted_iota(jnp.int32, (HEADS, LANES), 0) == lax.broadcasted_iota(jnp.int32, (HEADS, LANES), 1) // KEYS
    spread = jnp.where(spread, 1.0, 0.0).astype(BF16)
    for m in range(2):
        wr_s[m] = lax.dot_general(
            wb_ref[m], spread, (((0,), (0,)), ((), ())), preferred_element_type=F32
        ).astype(BF16)

    def remote(src, dst, send, recv, device):
        return pltpu.make_async_remote_copy(
            src_ref=src, dst_ref=dst, send_sem=send, recv_sem=recv,
            device_id=device, device_id_type=MESH,
        )

    def col_slice(which):
        return pl.ds(pl.multiple_of(which * cols_t, cols_t), cols_t)

    def row_slice(which):
        return pl.ds(pl.multiple_of(which * rows_t, rows_t), rows_t)

    def send_a1(o, carry):
        to = lax.rem(c + o, key_n)
        remote(x_ref.at[pl.ds(to * per, per)], x1.at[:, col_slice(c)], a1_send.at[o], a1_recv.at[o], (r, to)).start()
        return carry

    def wait_a1(o, carry):
        to = lax.rem(c + key_n - o, key_n)
        copy = remote(x_ref.at[pl.ds(to * per, per)], x1.at[:, col_slice(to)], a1_send.at[o], a1_recv.at[o], (r, to))
        copy.wait_send()
        copy.wait_recv()
        return carry

    size = {"y": y_n, "z": z_n, "x": x_n}
    place = {"y": y, "z": z, "x": xx}

    def device(which_core, **at):
        at = {**place, **at}
        return (at["y"] * 2 + which_core, at["z"] * x_n + at["x"])

    def shifted(axis, d):
        return lax.rem(place[axis] + d, size[axis])

    class Gather:
        def __init__(self, buf, send, recv, axes):
            self.buf, self.send, self.recv = buf, send, recv
            self.first, self.others = axes[0], axes[1:]
            self.parts = size[axes[0]]
            self.turns = size[axes[1]] - 1

        def block(self, which_core, **at):
            at = {**place, **at}
            return self.buf.at[at["y"], which_core, at["z"], at["x"]]

        def copy(self, slot, ref, to):
            return remote(ref, ref, self.send.at[slot], self.recv.at[slot], to)

        def line(self, p, which_core, **at):
            u, v = self.others if p % 2 == 0 else self.others[::-1]
            return self.block(which_core, **{self.first: p, u: slice(None), v: at.get("v", place[v])})

        def one(self, d, out):
            near = shifted(self.first, size[self.first] - d)
            if out:
                return self.copy(d - 1, self.block(core), device(core, **{self.first: shifted(self.first, d)}))
            return self.copy(d - 1, self.block(core, **{self.first: near}), device(core, **{self.first: near}))

        def two(self, p, d, out):
            u = self.others[p % 2]
            slot = self.parts - 1 + p * self.turns + d - 1
            near = shifted(u, size[u] - d)
            if out:
                return self.copy(slot, self.block(core, **{self.first: p}), device(core, **{u: shifted(u, d)}))
            return self.copy(slot, self.block(core, **{self.first: p, u: near}), device(core, **{u: near}))

        def three(self, p, d, out):
            v = self.others[1 - p % 2]
            slot = self.parts - 1 + (self.parts + p) * self.turns + d - 1
            near = shifted(v, size[v] - d)
            if out:
                return self.copy(slot, self.line(p, core), device(core, **{v: shifted(v, d)}))
            return self.copy(slot, self.line(p, core, v=near), device(core, **{v: near}))

        def mate(self, p, d, out):
            v = self.others[1 - p % 2]
            slot = self.parts - 1 + 2 * self.parts * self.turns + p * (self.turns + 1) + d
            near = shifted(v, size[v] - d)
            return self.copy(slot, self.line(p, core if out else 1 - core, v=near), device(1 - core))

        def steps(self):
            return range(1, self.turns + 1)

        def start_one(self):
            for d in range(1, self.parts):
                self.one(d, True).start()

        def start_two(self, h):
            for d in range(1, self.parts):
                near = shifted(self.first, self.parts - d)

                @pl.when(near // (self.parts // 2) == h)
                def _(d=d):
                    self.one(d, False).wait_recv()

            for p in self.half(h):
                for d in self.steps():
                    self.two(p, d, True).start()

        def half(self, h):
            return range(h * self.parts // 2, (h + 1) * self.parts // 2)

        def start_three(self, h):
            for p in self.half(h):
                for d in self.steps():
                    self.two(p, d, False).wait_recv()
                for d in self.steps():
                    self.three(p, d, True).start()
                self.mate(p, 0, True).start()

        def pass_on(self, h):
            for d in self.steps():
                for p in self.half(h):
                    self.three(p, d, False).wait_recv()
                    self.mate(p, d, True).start()

        def finish(self, h):
            for p in self.half(h):
                for d in range(self.turns + 1):
                    self.mate(p, d, False).wait_recv()

        def drain(self):
            for d in range(1, self.parts):
                self.one(d, True).wait_send()
            for p in range(self.parts):
                for d in self.steps():
                    self.two(p, d, True).wait_send()
                    self.three(p, d, True).wait_send()
                for d in range(self.turns + 1):
                    self.mate(p, d, True).wait_send()

    lane_q = lax.broadcasted_iota(jnp.int32, (KEYS, LANES), 1)

    def prepare(m, xs, i):
        normed = layer_norm(xs[i].astype(F32), gain_ref[m : m + 1], shift_ref[m : m + 1]).astype(BF16)

        def project(part):
            return jnp.dot(normed, wp_ref[m, :, part * LANES : (part + 1) * LANES], preferred_element_type=F32)

        q_s[i] = (project(0) * HEAD**-0.5).astype(BF16)
        k = project(1).astype(BF16)
        v = project(2).astype(BF16)
        g_s[i] = jax.nn.sigmoid(project(3) + gb_ref[m : m + 1])
        for g in range(groups):
            kg = k[g * KEYS : (g + 1) * KEYS]
            vg = v[g * KEYS : (g + 1) * KEYS]
            for h in range(HEADS):
                mine = lane_q // HEAD == h
                at = g * LANES + h * KEYS
                k_s[i, at : at + KEYS, :] = jnp.where(mine, kg, jnp.zeros_like(kg))
                v_s[i, at : at + KEYS, :LANES] = jnp.where(mine, vg, jnp.zeros_like(vg))

    width = groups * LANES

    def score_chunk(row, at, s_s, n, top):
        s = lax.dot_general(
            q_s[row, at, :], k_s[row, n : n + CHUNK, :], (((1,), (1,)), ((), ())), preferred_element_type=F32
        )
        s = s + bias_s[at, n : n + CHUNK]
        s_s[:, n : n + CHUNK] = s
        for t in range(0, CHUNK, LANES):
            part = s[:, t : t + LANES]
            top = part if top is None else jnp.maximum(top, part)
        return top

    def weight_chunk(s_s, p_s, n, top):
        p_s[:, n : n + CHUNK] = jnp.exp2((s_s[:, n : n + CHUNK] - top) * LOG2E).astype(BF16)

    def attend(m, unit_done, hooks):
        units = 2 * per

        def where(unit):
            return lax.rem(unit, per), pl.ds(pl.multiple_of(unit // per * half_t, half_t), half_t)

        def scores(unit, s_s, slot, before=None):
            row, at = where(unit)
            top = None
            if before is not None:
                s_b, p_b, slot_b = before
                top_b = jnp.concatenate([top_s[slot_b]] * (CHUNK // LANES), axis=1)
            for n in range(0, width, CHUNK):
                if before is not None:
                    weight_chunk(s_b, p_b, n, top_b)
                top = score_chunk(row, at, s_s, n, top)
            top_s[slot] = head_max(top, lane)

        def weights(s_s, p_s, slot):
            top = jnp.concatenate([top_s[slot]] * (CHUNK // LANES), axis=1)
            for n in range(0, width, CHUNK):
                weight_chunk(s_s, p_s, n, top)

        def values(unit, p_s):
            row, at = where(unit)
            total = jnp.dot(p_s[...], v_s[row], preferred_element_type=F32)
            gated = (total[:, :LANES] / total[:, LANES:] * g_s[row, at, :]).astype(BF16)
            update = jnp.dot(gated, wo_ref[m], preferred_element_type=F32)
            unit_done(row, unit // per, at, update)

        scores(0, s_even, 0)

        def pair(t, carry):
            unit = 2 * t

            def run_hooks(odd):
                for after, hook in hooks.items():
                    if after % 2 == odd:
                        pl.when(t == after // 2)(hook)

            scores(unit + 1, s_odd, 1, (s_even, p_even, 0))
            values(unit, p_even)
            run_hooks(0)

            @pl.when(t < per - 1)
            def _():
                scores(unit + 2, s_even, 0, (s_odd, p_odd, 1))
                values(unit + 1, p_odd)

            @pl.when(t == per - 1)
            def _():
                weights(s_odd, p_odd, 1)
                values(unit + 1, p_odd)

            run_hooks(1)
            return carry

        lax.fori_loop(0, per, pair, 0)

    x_copy.wait()
    tile_f[...] = layer_norm(x_ref[...].astype(F32), gain_ref[0:1], shift_ref[0:1])

    def pick(m, k):
        return jnp.where(lane_k % KEYS == k, wr_s[m], jnp.zeros((LANES, LANES), BF16))

    acc = jnp.zeros((rows_t, LANES), F32)
    for k in range(0, cols_t, 2):
        left = jnp.concatenate([tile_f[:, k, :], tile_f[:, k + 1, :]], axis=1).astype(BF16)
        right = jnp.concatenate([pick(0, k), pick(0, k + 1)], axis=0)
        acc = acc + jnp.dot(left, right, preferred_element_type=F32)
    bias_a[y, core, z, xx] = acc.astype(BF16)
    pl.semaphore_wait(barrier, key_n - 1 + row_n - 1)

    def more(m, xs, lo, hi):
        def one(i, carry):
            prepare(m, xs, i)
            return carry

        lax.fori_loop(lo, hi, one, 0)

    def widen_one(h):
        def widen(g, carry):
            at = pl.ds(pl.multiple_of(g * LANES, LANES), LANES)
            masked = key_bias(g)
            for rr in range(h * row_n // 2, (h + 1) * row_n // 2):
                block = bias_a[rr // 2, rr % 2, g // x_n, lax.rem(g, x_n)].astype(F32)
                bias_s[rr * rows_t : (rr + 1) * rows_t, at] = block + masked
            return carry

        lax.fori_loop(0, key_n, widen, 0)

    moves = Gather(bias_a, ga_send, ga_recv, "yzx")
    moves.start_one()
    lax.fori_loop(1, key_n, send_a1, 0)
    x1[:, col_slice(c)] = x_ref[pl.ds(c * per, per)]
    lax.fori_loop(0, per, put_ones, 0)
    for copy in w_copies:
        copy.wait()
    moves.start_two(0)
    moves.start_three(0)
    lax.fori_loop(1, key_n, wait_a1, 0)
    moves.start_two(1)
    more(0, x1, 0, per)
    moves.pass_on(0)
    moves.start_three(1)
    moves.finish(0)
    widen_one(0)

    def a2_copy(i, n, to, frm):
        return remote(
            as1.at[pl.ds(i, n), col_slice(to)], t2.at[pl.ds(frm * per + i, n)], a2_send.at[to], a2_recv.at[frm], (r, to)
        )

    def unit_one(i, h, at, update):
        keep = kept(h * half_t, rows_t * r + per * c + i, half_t)
        as1[i, at, :] = (x1[i, at, :].astype(F32) + keep * update).astype(BF16)

        def send(o, inner):
            to = h * (key_n // 2) + lax.rem(c + o, key_n // 2)

            @pl.when(to != c)
            def _():
                a2_copy(i, 1, to, c).start()

            return inner

        lax.fori_loop(0, key_n // 2, send, 0)

    def between_one():
        moves.finish(1)
        widen_one(1)

    def sent_a2(o, carry):
        a2_copy(0, per, lax.rem(c + o, key_n), c).wait_send()
        return carry

    def wait_a2(o, carry):
        frm = lax.rem(c + key_n - o, key_n)
        copy = remote(
            as1.at[pl.ds(0, per), col_slice(c)], t2.at[pl.ds(frm * per, per)], a2_send.at[frm], a2_recv.at[frm], (r, frm)
        )
        copy.wait_recv()
        return carry

    moves_two = Gather(bias_b, gb_send, gb_recv, "zyx")
    halves = rows_t // KEYS

    def b2_row(a, o, to):
        return remote(sb.at[to * per + a], x2.at[a, row_slice(r)], b2_send.at[o], b2_recv.at[a], (to, c))

    def b2_own(a):
        return pltpu.make_async_copy(sb.at[r * per + a], x2.at[a, row_slice(r)], b2_recv.at[a])

    def send_b2(a, carry):
        def send(o, inner):
            b2_row(a, o, lax.rem(r + o, row_n)).start()
            return inner

        lax.fori_loop(1, row_n, send, 0)
        b2_own(a).start()
        return carry

    def wait_b2(a):
        pltpu.make_async_copy(x2.at[a], x2.at[a], b2_recv.at[a]).wait()

    def sent_b2(o, carry):
        to = lax.rem(r + o, row_n)
        rows_out = sb.at[pl.ds(to * per, per)]
        remote(rows_out, rows_out, b2_send.at[o], b2_recv.at[0], (to, c)).wait_send()
        return carry

    def second_whole():
        lax.fori_loop(1, key_n, wait_a2, 0)
        t2[pl.ds(per * c, per)] = as1[:, col_slice(c)]

    def second_bias():
        tile_f[...] = layer_norm(t2[...].astype(F32), gain_ref[1:2], shift_ref[1:2])
        acc = jnp.zeros((rows_t, LANES), F32)
        for k in range(0, KEYS, 2):
            left = jnp.concatenate(
                [jnp.concatenate([tile_f[h * KEYS + kk] for h in range(halves)], axis=0) for kk in (k, k + 1)], axis=1
            ).astype(BF16)
            right = jnp.concatenate([pick(1, k), pick(1, k + 1)], axis=0)
            acc = acc + jnp.dot(left, right, preferred_element_type=F32)
        bias_b[y, core, z, xx] = acc.astype(BF16)
        moves_two.start_one()

    early = z < z_n // 2
    late = jnp.logical_not(early)

    def early_bias():
        @pl.when(early)
        def _():
            second_whole()
            second_bias()

    attend(0, unit_one, {per - 3: lambda: moves.pass_on(1), per - 2: between_one, 2 * per - 2: early_bias})
    pl.when(late)(second_whole)
    tile_f[...] = t2[...].astype(F32)
    for j in range(cols_t):
        sb[j] = tile_f[:, j, :].astype(BF16)
    lax.fori_loop(0, per, send_b2, 0)
    moves_two.start_two(0)
    pl.when(late)(second_bias)
    moves_two.start_three(0)
    wait_b2(0)
    prepare(1, x2, 0)
    moves_two.start_two(1)

    def late_row(a, carry):
        wait_b2(a)
        prepare(1, x2, a)
        return carry

    lax.fori_loop(1, per, late_row, 0)
    moves_two.pass_on(0)
    moves_two.start_three(1)
    moves_two.finish(0)

    def widen_two(h):
        def widen(g, carry):
            for gg in range(row_n * halves):
                rr, hh = gg // halves, gg % halves
                block = bias_b[rr // 2, rr % 2, g // x_n, lax.rem(g, x_n), hh * KEYS : (hh + 1) * KEYS, :].astype(F32)
                bias_s[col_slice(g), gg * LANES : (gg + 1) * LANES] = block + key_bias(gg)
            return carry

        lax.fori_loop(h * key_n // 2, (h + 1) * key_n // 2, widen, 0)

    widen_two(0)

    def c2_copy(i, n, to, frm):
        return remote(
            np2.at[pl.ds(i, n), row_slice(to)], fin.at[pl.ds(frm * per + i, n)], c2_send.at[to], c2_recv.at[frm], (to, c)
        )

    def unit_two(i, h, at, update):
        keep = kept(h * half_t, cols_t * c + per * r + i, half_t)
        update = (keep * update).astype(BF16).astype(F32)
        np2[i, at, :] = (x2[i, at, :].astype(F32) + update).astype(BF16)

        def send(o, inner):
            to = h * (row_n // 2) + lax.rem(r + o, row_n // 2)

            @pl.when(to != r)
            def _():
                c2_copy(i, 1, to, r).start()

            return inner

        lax.fori_loop(0, row_n // 2, send, 0)

    def between_two():
        moves_two.finish(1)
        widen_two(1)

    attend(1, unit_two, {per - 3: lambda: moves_two.pass_on(1), per - 2: between_two})
    fin[pl.ds(per * r, per)] = np2[:, row_slice(r)]
    moves.drain()
    moves_two.drain()
    lax.fori_loop(1, key_n, sent_a2, 0)
    lax.fori_loop(1, row_n, sent_b2, 0)

    def wait_c2(o, carry):
        c2_copy(0, per, lax.rem(r + o, row_n), r).wait_send()
        frm = lax.rem(r + row_n - o, row_n)
        copy = remote(
            np2.at[pl.ds(0, per), row_slice(r)], fin.at[pl.ds(frm * per, per)], c2_send.at[frm], c2_recv.at[frm], (frm, c)
        )
        copy.wait_recv()
        return carry

    lax.fori_loop(1, row_n, wait_c2, 0)


def local(row_n, key_n, pair_rep, token_mask, norm_gain, norm_shift, w_proj, w_bias, gate_bias, w_out):
    rows_t, cols_t, channels = pair_rep.shape
    tokens = token_mask.shape[0]
    per = tokens // (row_n * key_n)
    groups = tokens // KEYS
    width = groups * LANES
    y_n, z_n = row_n // 2, int(round(key_n**0.5))
    slots = y_n - 1 + 2 * y_n * (z_n - 1) + y_n * z_n
    vmem, dma = pltpu.VMEM, pltpu.SemaphoreType.DMA
    buf = (y_n, 2, z_n, z_n, rows_t, LANES)
    turned = pl.pallas_call(
        functools.partial(kernel, tokens, row_n, key_n),
        out_shape=jax.ShapeDtypeStruct((cols_t, rows_t, channels), BF16),
        in_specs=[pl.BlockSpec(memory_space=pl.ANY if i in (0, 4, 7) else pltpu.VMEM) for i in range(8)],
        out_specs=pl.BlockSpec(memory_space=pltpu.VMEM),
        scratch_shapes=[
            vmem((per, tokens, LANES), BF16),
            vmem((per, tokens, LANES), BF16),
            vmem((per, tokens, LANES), BF16),
            vmem((per, tokens, LANES), BF16),
            vmem((rows_t, cols_t, LANES), BF16),
            vmem((cols_t, rows_t, LANES), BF16),
            vmem((rows_t, cols_t, LANES), F32),
            vmem(buf, BF16),
            vmem(buf, BF16),
            vmem((tokens, width), F32),
            vmem((per, tokens, LANES), BF16),
            vmem((per, width, LANES), BF16),
            vmem((per, width, 2 * LANES), BF16),
            vmem((per, tokens, LANES), F32),
            vmem((tokens // 2, width), F32),
            vmem((tokens // 2, width), F32),
            vmem((tokens // 2, width), BF16),
            vmem((tokens // 2, width), BF16),
            vmem((2, tokens // 2, LANES), F32),
            vmem((2, LANES, LANES), BF16),
            vmem((rows_t, cols_t, LANES), BF16),
            vmem(w_proj.shape, BF16),
            vmem(w_out.shape, BF16),
            dma((3,)),
            dma((key_n,)), dma((key_n,)), dma((key_n,)), dma((key_n,)),
            dma((row_n,)), dma((row_n,)), dma((row_n,)), dma((row_n,)),
            dma((slots,)), dma((slots,)), dma((slots,)), dma((slots,)),
        ],
        compiler_params=pltpu.CompilerParams(
            collective_id=0, has_side_effects=True, vmem_limit_bytes=56 * 2**20
        ),
        name="triangle_attention",
    )(
        pair_rep, token_mask.reshape(-1, min(tokens, LANES)), norm_gain, norm_shift, w_proj, w_bias.transpose(0, 2, 1), gate_bias,
        w_out,
    )
    return turned.transpose(1, 0, 2)


def solution(mesh):
    row_n, key_n = mesh.shape["rows"], mesh.shape["keys"]
    in_specs = (P("rows", "keys", None), P(), P(), P(), P(), P(), P(), P())
    out_specs = P("rows", "keys", None)
    return jax.shard_map(
        functools.partial(local, row_n, key_n), mesh=mesh, in_specs=in_specs, out_specs=out_specs, check_vma=False
    )
```

```python
import functools

import jax
import jax.numpy as jnp
from jax import lax
from jax.experimental import pallas as pl
from jax.experimental.pallas import tpu as pltpu
from jax.sharding import PartitionSpec as P

MESH = pl.DeviceIdType.MESH
LOG2E = 1.4426950408889634
F32 = jnp.float32
BF16 = jnp.bfloat16
KEYS = 32
HEADS = 4
HEAD = 32
LANES = 128
CHUNK = 256


def layer_norm(values, gain, shift):
    center = jnp.mean(values, axis=-1, keepdims=True)
    moved = values - center
    spread = jnp.mean(moved * moved, axis=-1, keepdims=True)
    return moved * lax.rsqrt(spread + 1e-05) * gain + shift


def head_max(m, lane):
    for step in (16, 8, 4, 2, 1):
        below = pltpu.roll(m, step, 1)
        above = pltpu.roll(m, LANES - step, 1)
        m = jnp.maximum(m, jnp.where((lane & step) != 0, below, above))
    return m


def kernel(
    tokens, row_n, key_n,
    x_hbm, mask_ref, gain_ref, shift_ref, wp_hbm, wb_ref, gb_ref, wo_hbm,
    fin,
    x1, x2, as1, np2, t2, sb, tile_f, bias_a, bias_b, bias_s, q_s, k_s, v_s, g_s,
    s_even, s_odd, p_even, p_odd, top_s, wr_s, x_ref, wp_ref, wo_ref, x_sem,
    a1_send, a1_recv, a2_send, a2_recv, b2_send, b2_recv, c2_send, c2_recv,
    ga_send, ga_recv, gb_send, gb_recv,
):
    rows_t, cols_t = tokens // row_n, tokens // key_n
    per = tokens // (row_n * key_n)
    groups = tokens // KEYS
    y_n = row_n // 2
    z_n = x_n = int(round(key_n**0.5))
    half_t = tokens // 2
    r, c = lax.axis_index("rows"), lax.axis_index("keys")
    y, core = r // 2, r % 2
    z, xx = c // x_n, c % x_n
    lane = lax.broadcasted_iota(jnp.int32, (1, LANES), 1)

    barrier = pltpu.get_barrier_semaphore()
    x_copy = pltpu.make_async_copy(x_hbm, x_ref, x_sem.at[0])
    x_copy.start()
    w_copies = (
        pltpu.make_async_copy(wp_hbm, wp_ref, x_sem.at[1]),
        pltpu.make_async_copy(wo_hbm, wo_ref, x_sem.at[2]),
    )
    for copy in w_copies:
        copy.start()

    def greet_keys(o, carry):
        pl.semaphore_signal(barrier, inc=1, device_id=(r, lax.rem(c + o, key_n)), device_id_type=MESH)
        return carry

    def greet_rows(o, carry):
        pl.semaphore_signal(barrier, inc=1, device_id=(lax.rem(r + o, row_n), c), device_id_type=MESH)
        return carry

    lax.fori_loop(1, key_n, greet_keys, 0)
    lax.fori_loop(1, row_n, greet_rows, 0)

    def greet_planes(o, carry):
        far = lax.rem(y + 1 + o // (z_n - 1), y_n) * 2 + core
        step = 1 + o % (z_n - 1)
        pl.semaphore_signal(
            barrier, inc=1, device_id=(far, lax.rem(z + step, z_n) * x_n + xx), device_id_type=MESH
        )
        pl.semaphore_signal(
            barrier, inc=1, device_id=(far, z * x_n + lax.rem(xx + step, x_n)), device_id_type=MESH
        )
        return carry

    planes = (y_n - 1) * (z_n - 1)
    lax.fori_loop(0, planes, greet_planes, 0)

    real = jnp.sum(mask_ref[...], keepdims=True)

    def key_bias(g):
        key = g * KEYS + lane % KEYS
        return jnp.where(key < real, 0.0, -1000000000.0)

    def kept(first, token, count):
        at = first + lax.broadcasted_iota(jnp.int32, (count, LANES), 0)
        return jnp.where(jnp.logical_and(at < real, token < real), 1.0, 0.0)

    lane_k = lax.broadcasted_iota(jnp.int32, (LANES, LANES), 1)
    sub_k = lax.broadcasted_iota(jnp.int32, (LANES, LANES), 0)
    ones = jnp.where(lane_k // HEAD == sub_k // KEYS, 1.0, 0.0).astype(BF16)

    def put_ones(i, carry):
        for g in range(groups):
            v_s[i, g * LANES : (g + 1) * LANES, LANES:] = ones
        return carry

    spread = lax.broadcasted_iota(jnp.int32, (HEADS, LANES), 0) == lax.broadcasted_iota(jnp.int32, (HEADS, LANES), 1) // KEYS
    spread = jnp.where(spread, 1.0, 0.0).astype(BF16)
    for m in range(2):
        wr_s[m] = lax.dot_general(
            wb_ref[m], spread, (((0,), (0,)), ((), ())), preferred_element_type=F32
        ).astype(BF16)

    def remote(src, dst, send, recv, device):
        return pltpu.make_async_remote_copy(
            src_ref=src, dst_ref=dst, send_sem=send, recv_sem=recv,
            device_id=device, device_id_type=MESH,
        )

    def col_slice(which):
        return pl.ds(pl.multiple_of(which * cols_t, cols_t), cols_t)

    def row_slice(which):
        return pl.ds(pl.multiple_of(which * rows_t, rows_t), rows_t)

    def send_a1(o, carry):
        to = lax.rem(c + o, key_n)
        remote(x_ref.at[pl.ds(to * per, per)], x1.at[:, col_slice(c)], a1_send.at[o], a1_recv.at[o], (r, to)).start()
        return carry

    def wait_a1(o, carry):
        to = lax.rem(c + key_n - o, key_n)
        copy = remote(x_ref.at[pl.ds(to * per, per)], x1.at[:, col_slice(to)], a1_send.at[o], a1_recv.at[o], (r, to))
        copy.wait_send()
        copy.wait_recv()
        return carry

    size = {"y": y_n, "z": z_n, "x": x_n}
    place = {"y": y, "z": z, "x": xx}

    def device(which_core, **at):
        at = {**place, **at}
        return (at["y"] * 2 + which_core, at["z"] * x_n + at["x"])

    def shifted(axis, d):
        return lax.rem(place[axis] + d, size[axis])

    class Gather:
        def __init__(self, buf, send, recv, axes):
            self.buf, self.send, self.recv = buf, send, recv
            self.first, self.others = axes[0], axes[1:]
            self.parts = size[axes[0]]
            self.turns = size[axes[1]] - 1

        def block(self, which_core, **at):
            at = {**place, **at}
            return self.buf.at[at["y"], which_core, at["z"], at["x"]]

        def copy(self, slot, ref, to):
            return remote(ref, ref, self.send.at[slot], self.recv.at[slot], to)

        def line(self, p, which_core, **at):
            u, v = self.others if p % 2 == 0 else self.others[::-1]
            return self.block(which_core, **{self.first: p, u: slice(None), v: at.get("v", place[v])})

        def one(self, o):
            first, (a, b) = self.first, self.others
            odd = place[first] % 2
            n = self.turns + 1
            at = {
                first: lax.rem(place[first] + o // n, self.parts),
                a: lax.rem(place[a] + (o % n) * (1 - odd), size[a]),
                b: lax.rem(place[b] + (o % n) * odd, size[b]),
            }
            return self.copy(o - 1, self.block(core), device(core, **at))

        def wait_one(self, p):
            u = self.others[p % 2]
            away = lax.rem(place[self.first] + self.parts - p, self.parts)
            for d in range(self.turns + 1):
                at = {self.first: p, u: shifted(u, size[u] - d)}
                arrived = self.copy(away * (self.turns + 1) + d - 1, self.block(core, **at), device(core, **at))
                if d:
                    arrived.wait_recv()
                else:
                    pl.when(away != 0)(arrived.wait_recv)

        def three(self, p, d, out):
            v = self.others[1 - p % 2]
            slot = self.parts * (self.turns + 1) - 1 + p * self.turns + d - 1
            near = shifted(v, size[v] - d)
            if out:
                return self.copy(slot, self.line(p, core), device(core, **{v: shifted(v, d)}))
            return self.copy(slot, self.line(p, core, v=near), device(core, **{v: near}))

        def mate(self, p, d, out):
            v = self.others[1 - p % 2]
            slot = self.parts * (self.turns + 1) - 1 + self.parts * self.turns + p * (self.turns + 1) + d
            near = shifted(v, size[v] - d)
            return self.copy(slot, self.line(p, core if out else 1 - core, v=near), device(1 - core))

        def steps(self):
            return range(1, self.turns + 1)

        def start_one(self):
            def send(o, carry):
                self.one(o).start()
                return carry

            lax.fori_loop(1, self.parts * (self.turns + 1), send, 0)

        def half(self, h):
            return range(h * self.parts // 2, (h + 1) * self.parts // 2)

        def start_three(self, h):
            for p in self.half(h):
                self.wait_one(p)
                for d in self.steps():
                    self.three(p, d, True).start()
                self.mate(p, 0, True).start()

        def pass_on(self, h):
            for d in self.steps():
                for p in self.half(h):
                    self.three(p, d, False).wait_recv()
                    self.mate(p, d, True).start()

        def finish(self, h):
            for p in self.half(h):
                for d in range(self.turns + 1):
                    self.mate(p, d, False).wait_recv()

        def drain(self):
            def sent(o, carry):
                self.one(o).wait_send()
                return carry

            lax.fori_loop(1, self.parts * (self.turns + 1), sent, 0)
            for p in range(self.parts):
                for d in self.steps():
                    self.three(p, d, True).wait_send()
                for d in range(self.turns + 1):
                    self.mate(p, d, True).wait_send()

    lane_q = lax.broadcasted_iota(jnp.int32, (KEYS, LANES), 1)

    def prepare(m, xs, i):
        normed = layer_norm(xs[i].astype(F32), gain_ref[m : m + 1], shift_ref[m : m + 1]).astype(BF16)

        def project(part):
            return jnp.dot(normed, wp_ref[m, :, part * LANES : (part + 1) * LANES], preferred_element_type=F32)

        q_s[i] = (project(0) * HEAD**-0.5).astype(BF16)
        k = project(1).astype(BF16)
        v = project(2).astype(BF16)
        g_s[i] = jax.nn.sigmoid(project(3) + gb_ref[m : m + 1])
        for g in range(groups):
            kg = k[g * KEYS : (g + 1) * KEYS]
            vg = v[g * KEYS : (g + 1) * KEYS]
            for h in range(HEADS):
                mine = lane_q // HEAD == h
                at = g * LANES + h * KEYS
                k_s[i, at : at + KEYS, :] = jnp.where(mine, kg, jnp.zeros_like(kg))
                v_s[i, at : at + KEYS, :LANES] = jnp.where(mine, vg, jnp.zeros_like(vg))

    width = groups * LANES

    def score_chunk(row, at, s_s, n, top):
        s = lax.dot_general(
            q_s[row, at, :], k_s[row, n : n + CHUNK, :], (((1,), (1,)), ((), ())), preferred_element_type=F32
        )
        s = s + bias_s[at, n : n + CHUNK]
        s_s[:, n : n + CHUNK] = s
        for t in range(0, CHUNK, LANES):
            part = s[:, t : t + LANES]
            top = part if top is None else jnp.maximum(top, part)
        return top

    def weight_chunk(s_s, p_s, n, top):
        p_s[:, n : n + CHUNK] = jnp.exp2((s_s[:, n : n + CHUNK] - top) * LOG2E).astype(BF16)

    def attend(m, unit_done, hooks):
        units = 2 * per

        def where(unit):
            return lax.rem(unit, per), pl.ds(pl.multiple_of(unit // per * half_t, half_t), half_t)

        def scores(unit, s_s, slot, before=None):
            row, at = where(unit)
            top = None
            if before is not None:
                s_b, p_b, slot_b = before
                top_b = jnp.concatenate([top_s[slot_b]] * (CHUNK // LANES), axis=1)
            for n in range(0, width, CHUNK):
                if before is not None:
                    weight_chunk(s_b, p_b, n, top_b)
                top = score_chunk(row, at, s_s, n, top)
            top_s[slot] = head_max(top, lane)

        def weights(s_s, p_s, slot):
            top = jnp.concatenate([top_s[slot]] * (CHUNK // LANES), axis=1)
            for n in range(0, width, CHUNK):
                weight_chunk(s_s, p_s, n, top)

        def values(unit, p_s):
            row, at = where(unit)
            total = jnp.dot(p_s[...], v_s[row], preferred_element_type=F32)
            gated = (total[:, :LANES] / total[:, LANES:] * g_s[row, at, :]).astype(BF16)
            update = jnp.dot(gated, wo_ref[m], preferred_element_type=F32)
            unit_done(row, unit // per, at, update)

        scores(0, s_even, 0)

        def pair(t, carry):
            unit = 2 * t

            def run_hooks(odd):
                for after, hook in hooks.items():
                    if after % 2 == odd:
                        pl.when(t == after // 2)(hook)

            scores(unit + 1, s_odd, 1, (s_even, p_even, 0))
            values(unit, p_even)
            run_hooks(0)

            @pl.when(t < per - 1)
            def _():
                scores(unit + 2, s_even, 0, (s_odd, p_odd, 1))
                values(unit + 1, p_odd)

            @pl.when(t == per - 1)
            def _():
                weights(s_odd, p_odd, 1)
                values(unit + 1, p_odd)

            run_hooks(1)
            return carry

        lax.fori_loop(0, per, pair, 0)

    x_copy.wait()
    tile_f[...] = layer_norm(x_ref[...].astype(F32), gain_ref[0:1], shift_ref[0:1])

    def pick(m, k):
        return jnp.where(lane_k % KEYS == k, wr_s[m], jnp.zeros((LANES, LANES), BF16))

    acc = jnp.zeros((rows_t, LANES), F32)
    for k in range(0, cols_t, 2):
        left = jnp.concatenate([tile_f[:, k, :], tile_f[:, k + 1, :]], axis=1).astype(BF16)
        right = jnp.concatenate([pick(0, k), pick(0, k + 1)], axis=0)
        acc = acc + jnp.dot(left, right, preferred_element_type=F32)
    bias_a[y, core, z, xx] = acc.astype(BF16)
    pl.semaphore_wait(barrier, key_n - 1 + row_n - 1 + 2 * planes)

    def more(m, xs, lo, hi):
        def one(i, carry):
            prepare(m, xs, i)
            return carry

        lax.fori_loop(lo, hi, one, 0)

    def widen_one(h):
        def widen(g, carry):
            at = pl.ds(pl.multiple_of(g * LANES, LANES), LANES)
            masked = key_bias(g)
            for rr in range(h * row_n // 2, (h + 1) * row_n // 2):
                block = bias_a[rr // 2, rr % 2, g // x_n, lax.rem(g, x_n)].astype(F32)
                bias_s[rr * rows_t : (rr + 1) * rows_t, at] = block + masked
            return carry

        lax.fori_loop(0, key_n, widen, 0)

    moves = Gather(bias_a, ga_send, ga_recv, "yzx")
    moves.start_one()
    lax.fori_loop(1, key_n, send_a1, 0)
    x1[:, col_slice(c)] = x_ref[pl.ds(c * per, per)]
    lax.fori_loop(0, per, put_ones, 0)
    for copy in w_copies:
        copy.wait()
    moves.start_three(0)
    lax.fori_loop(1, key_n, wait_a1, 0)
    more(0, x1, 0, 1)
    moves.start_three(1)
    more(0, x1, 1, per)
    moves.pass_on(0)
    moves.finish(0)
    widen_one(0)

    def a2_copy(i, n, to, frm):
        return remote(
            as1.at[pl.ds(i, n), col_slice(to)], t2.at[pl.ds(frm * per + i, n)], a2_send.at[to], a2_recv.at[frm], (r, to)
        )

    def unit_one(i, h, at, update):
        keep = kept(h * half_t, rows_t * r + per * c + i, half_t)
        as1[i, at, :] = (x1[i, at, :].astype(F32) + keep * update).astype(BF16)

        def send(o, inner):
            to = h * (key_n // 2) + lax.rem(c + o, key_n // 2)

            @pl.when(to != c)
            def _():
                a2_copy(i, 1, to, c).start()

            return inner

        lax.fori_loop(0, key_n // 2, send, 0)

    def between_one():
        moves.finish(1)
        widen_one(1)

    def sent_a2(o, carry):
        a2_copy(0, per, lax.rem(c + o, key_n), c).wait_send()
        return carry

    def wait_a2(o, carry):
        frm = lax.rem(c + key_n - o, key_n)
        copy = remote(
            as1.at[pl.ds(0, per), col_slice(c)], t2.at[pl.ds(frm * per, per)], a2_send.at[frm], a2_recv.at[frm], (r, frm)
        )
        copy.wait_recv()
        return carry

    moves_two = Gather(bias_b, gb_send, gb_recv, "zyx")
    halves = rows_t // KEYS

    def b2_row(a, o, to):
        return remote(sb.at[to * per + a], x2.at[a, row_slice(r)], b2_send.at[o], b2_recv.at[a], (to, c))

    def b2_own(a):
        return pltpu.make_async_copy(sb.at[r * per + a], x2.at[a, row_slice(r)], b2_recv.at[a])

    def send_b2(a, carry):
        def send(o, inner):
            b2_row(a, o, lax.rem(r + o, row_n)).start()
            return inner

        lax.fori_loop(1, row_n, send, 0)
        b2_own(a).start()
        return carry

    def wait_b2(a):
        pltpu.make_async_copy(x2.at[a], x2.at[a], b2_recv.at[a]).wait()

    def sent_b2(o, carry):
        to = lax.rem(r + o, row_n)
        rows_out = sb.at[pl.ds(to * per, per)]
        remote(rows_out, rows_out, b2_send.at[o], b2_recv.at[0], (to, c)).wait_send()
        return carry

    def second_whole():
        lax.fori_loop(1, key_n, wait_a2, 0)
        t2[pl.ds(per * c, per)] = as1[:, col_slice(c)]

    def second_bias():
        tile_f[...] = layer_norm(t2[...].astype(F32), gain_ref[1:2], shift_ref[1:2])
        acc = jnp.zeros((rows_t, LANES), F32)
        for k in range(0, KEYS, 2):
            left = jnp.concatenate(
                [jnp.concatenate([tile_f[h * KEYS + kk] for h in range(halves)], axis=0) for kk in (k, k + 1)], axis=1
            ).astype(BF16)
            right = jnp.concatenate([pick(1, k), pick(1, k + 1)], axis=0)
            acc = acc + jnp.dot(left, right, preferred_element_type=F32)
        bias_b[y, core, z, xx] = acc.astype(BF16)
        moves_two.start_one()

    early = z < z_n // 2
    late = jnp.logical_not(early)

    def early_bias():
        @pl.when(early)
        def _():
            second_whole()
            second_bias()

    attend(0, unit_one, {per - 3: lambda: moves.pass_on(1), per - 2: between_one, 2 * per - 2: early_bias})
    moves_two.start_three(0)
    @pl.when(late)
    def _():
        second_whole()
        second_bias()

    tile_f[...] = t2[...].astype(F32)
    for j in range(cols_t):
        sb[j] = tile_f[:, j, :].astype(BF16)
    lax.fori_loop(0, per, send_b2, 0)
    moves_two.pass_on(0)
    moves.drain()
    lax.fori_loop(1, key_n, sent_a2, 0)

    def late_row(a, carry):
        wait_b2(a)
        prepare(1, x2, a)
        return carry

    lax.fori_loop(0, 1, late_row, 0)
    moves_two.start_three(1)
    lax.fori_loop(1, per, late_row, 0)
    moves_two.finish(0)

    def widen_two(h):
        def widen(g, carry):
            for gg in range(row_n * halves):
                rr, hh = gg // halves, gg % halves
                block = bias_b[rr // 2, rr % 2, g // x_n, lax.rem(g, x_n), hh * KEYS : (hh + 1) * KEYS, :].astype(F32)
                bias_s[col_slice(g), gg * LANES : (gg + 1) * LANES] = block + key_bias(gg)
            return carry

        lax.fori_loop(h * key_n // 2, (h + 1) * key_n // 2, widen, 0)

    widen_two(0)

    def c2_copy(i, n, to, frm):
        return remote(
            np2.at[pl.ds(i, n), row_slice(to)], fin.at[pl.ds(frm * per + i, n)], c2_send.at[to], c2_recv.at[frm], (to, c)
        )

    def unit_two(i, h, at, update):
        keep = kept(h * half_t, cols_t * c + per * r + i, half_t)
        update = (keep * update).astype(BF16).astype(F32)
        np2[i, at, :] = (x2[i, at, :].astype(F32) + update).astype(BF16)

        def send(o, inner):
            to = h * (row_n // 2) + lax.rem(r + o, row_n // 2)

            @pl.when(to != r)
            def _():
                c2_copy(i, 1, to, r).start()

            return inner

        lax.fori_loop(0, row_n // 2, send, 0)

    def between_two():
        moves_two.finish(1)
        widen_two(1)

    attend(1, unit_two, {per - 3: lambda: moves_two.pass_on(1), per - 2: between_two})
    fin[pl.ds(per * r, per)] = np2[:, row_slice(r)]
    moves_two.drain()
    lax.fori_loop(1, row_n, sent_b2, 0)

    def wait_c2(o, carry):
        c2_copy(0, per, lax.rem(r + o, row_n), r).wait_send()
        frm = lax.rem(r + row_n - o, row_n)
        copy = remote(
            np2.at[pl.ds(0, per), row_slice(r)], fin.at[pl.ds(frm * per, per)], c2_send.at[frm], c2_recv.at[frm], (frm, c)
        )
        copy.wait_recv()
        return carry

    lax.fori_loop(1, row_n, wait_c2, 0)


def local(row_n, key_n, pair_rep, token_mask, norm_gain, norm_shift, w_proj, w_bias, gate_bias, w_out):
    rows_t, cols_t, channels = pair_rep.shape
    tokens = token_mask.shape[0]
    per = tokens // (row_n * key_n)
    groups = tokens // KEYS
    width = groups * LANES
    y_n, z_n = row_n // 2, int(round(key_n**0.5))
    slots = y_n - 1 + 2 * y_n * (z_n - 1) + y_n * z_n
    vmem, dma = pltpu.VMEM, pltpu.SemaphoreType.DMA
    buf = (y_n, 2, z_n, z_n, rows_t, LANES)
    turned = pl.pallas_call(
        functools.partial(kernel, tokens, row_n, key_n),
        out_shape=jax.ShapeDtypeStruct((cols_t, rows_t, channels), BF16),
        in_specs=[pl.BlockSpec(memory_space=pl.ANY if i in (0, 4, 7) else pltpu.VMEM) for i in range(8)],
        out_specs=pl.BlockSpec(memory_space=pltpu.VMEM),
        scratch_shapes=[
            vmem((per, tokens, LANES), BF16),
            vmem((per, tokens, LANES), BF16),
            vmem((per, tokens, LANES), BF16),
            vmem((per, tokens, LANES), BF16),
            vmem((rows_t, cols_t, LANES), BF16),
            vmem((cols_t, rows_t, LANES), BF16),
            vmem((rows_t, cols_t, LANES), F32),
            vmem(buf, BF16),
            vmem(buf, BF16),
            vmem((tokens, width), F32),
            vmem((per, tokens, LANES), BF16),
            vmem((per, width, LANES), BF16),
            vmem((per, width, 2 * LANES), BF16),
            vmem((per, tokens, LANES), F32),
            vmem((tokens // 2, width), F32),
            vmem((tokens // 2, width), F32),
            vmem((tokens // 2, width), BF16),
            vmem((tokens // 2, width), BF16),
            vmem((2, tokens // 2, LANES), F32),
            vmem((2, LANES, LANES), BF16),
            vmem((rows_t, cols_t, LANES), BF16),
            vmem(w_proj.shape, BF16),
            vmem(w_out.shape, BF16),
            dma((3,)),
            dma((key_n,)), dma((key_n,)), dma((key_n,)), dma((key_n,)),
            dma((row_n,)), dma((row_n,)), dma((row_n,)), dma((row_n,)),
            dma((slots,)), dma((slots,)), dma((slots,)), dma((slots,)),
        ],
        compiler_params=pltpu.CompilerParams(
            collective_id=0, has_side_effects=True, vmem_limit_bytes=56 * 2**20
        ),
        name="triangle_attention",
    )(
        pair_rep, token_mask.reshape(-1, min(tokens, LANES)), norm_gain, norm_shift, w_proj, w_bias.transpose(0, 2, 1), gate_bias,
        w_out,
    )
    return turned.transpose(1, 0, 2)


def solution(mesh):
    row_n, key_n = mesh.shape["rows"], mesh.shape["keys"]
    in_specs = (P("rows", "keys", None), P(), P(), P(), P(), P(), P(), P())
    out_specs = P("rows", "keys", None)
    return jax.shard_map(
        functools.partial(local, row_n, key_n), mesh=mesh, in_specs=in_specs, out_specs=out_specs, check_vma=False
    )
```

```python
import functools

import jax
import jax.numpy as jnp
from jax import lax
from jax.experimental import pallas as pl
from jax.experimental.pallas import tpu as pltpu
from jax.sharding import PartitionSpec as P

MESH = pl.DeviceIdType.MESH
LOG2E = 1.4426950408889634
F32 = jnp.float32
BF16 = jnp.bfloat16
KEYS = 32
HEADS = 4
HEAD = 32
LANES = 128
CHUNK = 256


def layer_norm(values, gain, shift):
    center = jnp.mean(values, axis=-1, keepdims=True)
    moved = values - center
    spread = jnp.mean(moved * moved, axis=-1, keepdims=True)
    return moved * lax.rsqrt(spread + 1e-05) * gain + shift


def head_max(m, lane):
    out = None
    for h in range(HEADS):
        mine = lane // KEYS == h
        largest = jnp.max(jnp.where(mine, m, -jnp.inf), axis=-1, keepdims=True)
        out = largest if out is None else jnp.where(mine, largest, out)
    return jnp.broadcast_to(out, m.shape)


def kernel(
    tokens, row_n, key_n,
    x_hbm, mask_ref, gain_ref, shift_ref, wp_hbm, wb_ref, gb_ref, wo_hbm,
    fin,
    x1, x2, as1, np2, t2, sb, tile_f, bias_a, bias_b, bias_s, q_s, k_s, v_s, g_s,
    s_even, s_odd, p_even, p_odd, top_s, wr_s, x_ref, wp_ref, wo_ref, x_sem,
    a1_send, a1_recv, a2_send, a2_recv, b2_send, b2_recv, c2_send, c2_recv,
    ga_send, ga_recv, gb_send, gb_recv,
):
    rows_t, cols_t = tokens // row_n, tokens // key_n
    per = tokens // (row_n * key_n)
    groups = tokens // KEYS
    y_n = row_n // 2
    z_n = x_n = int(round(key_n**0.5))
    half_t = tokens // 2
    r, c = lax.axis_index("rows"), lax.axis_index("keys")
    y, core = r // 2, r % 2
    z, xx = c // x_n, c % x_n
    lane = lax.broadcasted_iota(jnp.int32, (1, LANES), 1)

    barrier = pltpu.get_barrier_semaphore()
    x_copy = pltpu.make_async_copy(x_hbm, x_ref, x_sem.at[0])
    x_copy.start()
    w_copies = (
        pltpu.make_async_copy(wp_hbm, wp_ref, x_sem.at[1]),
        pltpu.make_async_copy(wo_hbm, wo_ref, x_sem.at[2]),
    )
    for copy in w_copies:
        copy.start()

    def greet_keys(o, carry):
        pl.semaphore_signal(barrier, inc=1, device_id=(r, lax.rem(c + o, key_n)), device_id_type=MESH)
        return carry

    def greet_rows(o, carry):
        pl.semaphore_signal(barrier, inc=1, device_id=(lax.rem(r + o, row_n), c), device_id_type=MESH)
        return carry

    lax.fori_loop(1, key_n, greet_keys, 0)
    lax.fori_loop(1, row_n, greet_rows, 0)

    def greet_planes(o, carry):
        far = lax.rem(y + 1 + o // (z_n - 1), y_n) * 2 + core
        step = 1 + o % (z_n - 1)
        pl.semaphore_signal(
            barrier, inc=1, device_id=(far, lax.rem(z + step, z_n) * x_n + xx), device_id_type=MESH
        )
        pl.semaphore_signal(
            barrier, inc=1, device_id=(far, z * x_n + lax.rem(xx + step, x_n)), device_id_type=MESH
        )
        return carry

    planes = (y_n - 1) * (z_n - 1)
    lax.fori_loop(0, planes, greet_planes, 0)

    real = jnp.sum(mask_ref[...], keepdims=True)

    def key_bias(g):
        key = g * KEYS + lane % KEYS
        return jnp.where(key < real, 0.0, -1000000000.0)

    def kept(first, token, count):
        at = first + lax.broadcasted_iota(jnp.int32, (count, LANES), 0)
        return jnp.where(jnp.logical_and(at < real, token < real), 1.0, 0.0)

    lane_k = lax.broadcasted_iota(jnp.int32, (LANES, LANES), 1)
    sub_k = lax.broadcasted_iota(jnp.int32, (LANES, LANES), 0)
    ones = jnp.where(lane_k // HEAD == sub_k // KEYS, 1.0, 0.0).astype(BF16)

    def put_ones(i, carry):
        for g in range(groups):
            v_s[i, g * LANES : (g + 1) * LANES, LANES:] = ones
        return carry

    spread = lax.broadcasted_iota(jnp.int32, (HEADS, LANES), 0) == lax.broadcasted_iota(jnp.int32, (HEADS, LANES), 1) // KEYS
    spread = jnp.where(spread, 1.0, 0.0).astype(BF16)
    for m in range(2):
        wr_s[m] = lax.dot_general(
            wb_ref[m], spread, (((0,), (0,)), ((), ())), preferred_element_type=F32
        ).astype(BF16)

    def remote(src, dst, send, recv, device):
        return pltpu.make_async_remote_copy(
            src_ref=src, dst_ref=dst, send_sem=send, recv_sem=recv,
            device_id=device, device_id_type=MESH,
        )

    def col_slice(which):
        return pl.ds(pl.multiple_of(which * cols_t, cols_t), cols_t)

    def row_slice(which):
        return pl.ds(pl.multiple_of(which * rows_t, rows_t), rows_t)

    def send_a1(o, carry):
        to = lax.rem(c + o, key_n)
        remote(x_ref.at[pl.ds(to * per, per)], x1.at[:, col_slice(c)], a1_send.at[o], a1_recv.at[o], (r, to)).start()
        return carry

    def wait_a1(o, carry):
        to = lax.rem(c + key_n - o, key_n)
        copy = remote(x_ref.at[pl.ds(to * per, per)], x1.at[:, col_slice(to)], a1_send.at[o], a1_recv.at[o], (r, to))
        copy.wait_send()
        copy.wait_recv()
        return carry

    size = {"y": y_n, "z": z_n, "x": x_n}
    place = {"y": y, "z": z, "x": xx}

    def device(which_core, **at):
        at = {**place, **at}
        return (at["y"] * 2 + which_core, at["z"] * x_n + at["x"])

    def shifted(axis, d):
        return lax.rem(place[axis] + d, size[axis])

    class Gather:
        def __init__(self, buf, send, recv, axes):
            self.buf, self.send, self.recv = buf, send, recv
            self.first, self.others = axes[0], axes[1:]
            self.parts = size[axes[0]]
            self.turns = size[axes[1]] - 1

        def block(self, which_core, **at):
            at = {**place, **at}
            return self.buf.at[at["y"], which_core, at["z"], at["x"]]

        def copy(self, slot, ref, to):
            return remote(ref, ref, self.send.at[slot], self.recv.at[slot], to)

        def line(self, p, which_core, **at):
            u, v = self.others if p % 2 == 0 else self.others[::-1]
            return self.block(which_core, **{self.first: p, u: slice(None), v: at.get("v", place[v])})

        def one(self, o):
            first, (a, b) = self.first, self.others
            odd = place[first] % 2
            n = self.turns + 1
            at = {
                first: lax.rem(place[first] + o // n, self.parts),
                a: lax.rem(place[a] + (o % n) * (1 - odd), size[a]),
                b: lax.rem(place[b] + (o % n) * odd, size[b]),
            }
            return self.copy(o - 1, self.block(core), device(core, **at))

        def wait_one(self, p):
            u = self.others[p % 2]
            away = lax.rem(place[self.first] + self.parts - p, self.parts)
            for d in range(self.turns + 1):
                at = {self.first: p, u: shifted(u, size[u] - d)}
                arrived = self.copy(away * (self.turns + 1) + d - 1, self.block(core, **at), device(core, **at))
                if d:
                    arrived.wait_recv()
                else:
                    pl.when(away != 0)(arrived.wait_recv)

        def three(self, p, d, out):
            v = self.others[1 - p % 2]
            slot = self.parts * (self.turns + 1) - 1 + p * self.turns + d - 1
            near = shifted(v, size[v] - d)
            if out:
                return self.copy(slot, self.line(p, core), device(core, **{v: shifted(v, d)}))
            return self.copy(slot, self.line(p, core, v=near), device(core, **{v: near}))

        def mate(self, p, d, out):
            v = self.others[1 - p % 2]
            slot = self.parts * (self.turns + 1) - 1 + self.parts * self.turns + p * (self.turns + 1) + d
            near = shifted(v, size[v] - d)
            return self.copy(slot, self.line(p, core if out else 1 - core, v=near), device(1 - core))

        def steps(self):
            return sorted(range(1, self.turns + 1), key=lambda d: min(d, self.turns + 1 - d))

        def start_one(self):
            def send(o, carry):
                self.one(o).start()
                return carry

            lax.fori_loop(1, self.parts * (self.turns + 1), send, 0)

        def half(self, h):
            return range(h * self.parts // 2, (h + 1) * self.parts // 2)

        def start_three(self, h):
            for p in self.half(h):
                self.wait_one(p)
                for d in self.steps():
                    self.three(p, d, True).start()
                self.mate(p, 0, True).start()

        def pass_on(self, h):
            for d in self.steps():
                for p in self.half(h):
                    self.three(p, d, False).wait_recv()
                    self.mate(p, d, True).start()

        def finish(self, h):
            for p in self.half(h):
                for d in range(self.turns + 1):
                    self.mate(p, d, False).wait_recv()

        def drain(self):
            def sent(o, carry):
                self.one(o).wait_send()
                return carry

            lax.fori_loop(1, self.parts * (self.turns + 1), sent, 0)
            for p in range(self.parts):
                for d in self.steps():
                    self.three(p, d, True).wait_send()
                for d in range(self.turns + 1):
                    self.mate(p, d, True).wait_send()

    lane_q = lax.broadcasted_iota(jnp.int32, (KEYS, LANES), 1)

    def prepare(m, xs, i):
        normed = layer_norm(xs[i].astype(F32), gain_ref[m : m + 1], shift_ref[m : m + 1]).astype(BF16)

        def project(part):
            return jnp.dot(normed, wp_ref[m, :, part * LANES : (part + 1) * LANES], preferred_element_type=F32)

        q_s[i] = (project(0) * HEAD**-0.5).astype(BF16)
        k = project(1).astype(BF16)
        v = project(2).astype(BF16)
        g_s[i] = jax.nn.sigmoid(project(3) + gb_ref[m : m + 1])
        for g in range(groups):
            kg = k[g * KEYS : (g + 1) * KEYS]
            vg = v[g * KEYS : (g + 1) * KEYS]
            for h in range(HEADS):
                mine = lane_q // HEAD == h
                at = g * LANES + h * KEYS
                k_s[i, at : at + KEYS, :] = jnp.where(mine, kg, jnp.zeros_like(kg))
                v_s[i, at : at + KEYS, :LANES] = jnp.where(mine, vg, jnp.zeros_like(vg))

    width = groups * LANES

    def score_chunk(row, at, s_s, n, top):
        s = lax.dot_general(
            q_s[row, at, :], k_s[row, n : n + CHUNK, :], (((1,), (1,)), ((), ())), preferred_element_type=F32
        )
        s = s + bias_s[at, n : n + CHUNK]
        s_s[:, n : n + CHUNK] = s
        for t in range(0, CHUNK, LANES):
            part = s[:, t : t + LANES]
            top = part if top is None else jnp.maximum(top, part)
        return top

    def weight_chunk(s_s, p_s, n, top):
        p_s[:, n : n + CHUNK] = jnp.exp2((s_s[:, n : n + CHUNK] - top) * LOG2E).astype(BF16)

    def attend(m, unit_done, hooks):
        units = 2 * per

        def where(unit):
            return lax.rem(unit, per), pl.ds(pl.multiple_of(unit // per * half_t, half_t), half_t)

        def scores(unit, s_s, slot, before=None):
            row, at = where(unit)
            top = None
            if before is not None:
                s_b, p_b, slot_b = before
                top_b = jnp.concatenate([top_s[slot_b]] * (CHUNK // LANES), axis=1)
            for n in range(0, width, CHUNK):
                if before is not None:
                    weight_chunk(s_b, p_b, n, top_b)
                top = score_chunk(row, at, s_s, n, top)
            top_s[slot] = head_max(top, lane)

        def weights(s_s, p_s, slot):
            top = jnp.concatenate([top_s[slot]] * (CHUNK // LANES), axis=1)
            for n in range(0, width, CHUNK):
                weight_chunk(s_s, p_s, n, top)

        def values(unit, p_s):
            row, at = where(unit)
            total = jnp.dot(p_s[...], v_s[row], preferred_element_type=F32)
            gated = (total[:, :LANES] / total[:, LANES:] * g_s[row, at, :]).astype(BF16)
            update = jnp.dot(gated, wo_ref[m], preferred_element_type=F32)
            unit_done(row, unit // per, at, update)

        scores(0, s_even, 0)

        def pair(t, carry):
            unit = 2 * t

            def run_hooks(odd):
                for after, hook in hooks.items():
                    if after % 2 == odd:
                        pl.when(t == after // 2)(hook)

            scores(unit + 1, s_odd, 1, (s_even, p_even, 0))
            values(unit, p_even)
            run_hooks(0)

            @pl.when(t < per - 1)
            def _():
                scores(unit + 2, s_even, 0, (s_odd, p_odd, 1))
                values(unit + 1, p_odd)

            @pl.when(t == per - 1)
            def _():
                weights(s_odd, p_odd, 1)
                values(unit + 1, p_odd)

            run_hooks(1)
            return carry

        lax.fori_loop(0, per, pair, 0)

    x_copy.wait()
    tile_f[...] = layer_norm(x_ref[...].astype(F32), gain_ref[0:1], shift_ref[0:1])

    def pick(m, k):
        return jnp.where(lane_k % KEYS == k, wr_s[m], jnp.zeros((LANES, LANES), BF16))

    acc = jnp.zeros((rows_t, LANES), F32)
    for k in range(0, cols_t, 2):
        left = jnp.concatenate([tile_f[:, k, :], tile_f[:, k + 1, :]], axis=1).astype(BF16)
        right = jnp.concatenate([pick(0, k), pick(0, k + 1)], axis=0)
        acc = acc + jnp.dot(left, right, preferred_element_type=F32)
    bias_a[y, core, z, xx] = acc.astype(BF16)
    pl.semaphore_wait(barrier, key_n - 1 + row_n - 1 + 2 * planes)

    def more(m, xs, lo, hi):
        def one(i, carry):
            prepare(m, xs, i)
            return carry

        lax.fori_loop(lo, hi, one, 0)

    def widen_one(h):
        def widen(g, carry):
            at = pl.ds(pl.multiple_of(g * LANES, LANES), LANES)
            masked = key_bias(g)
            for rr in range(h * row_n // 2, (h + 1) * row_n // 2):
                block = bias_a[rr // 2, rr % 2, g // x_n, lax.rem(g, x_n)].astype(F32)
                bias_s[rr * rows_t : (rr + 1) * rows_t, at] = block + masked
            return carry

        lax.fori_loop(0, key_n, widen, 0)

    moves = Gather(bias_a, ga_send, ga_recv, "yzx")
    moves.start_one()
    lax.fori_loop(1, key_n, send_a1, 0)
    x1[:, col_slice(c)] = x_ref[pl.ds(c * per, per)]
    lax.fori_loop(0, per, put_ones, 0)
    for copy in w_copies:
        copy.wait()
    moves.start_three(0)
    lax.fori_loop(1, key_n, wait_a1, 0)
    more(0, x1, 0, 1)
    moves.start_three(1)
    more(0, x1, 1, per)
    moves.pass_on(0)
    moves.finish(0)
    widen_one(0)

    def a2_copy(i, n, to, frm):
        return remote(
            as1.at[pl.ds(i, n), col_slice(to)], t2.at[pl.ds(frm * per + i, n)], a2_send.at[to], a2_recv.at[frm], (r, to)
        )

    def unit_one(i, h, at, update):
        keep = kept(h * half_t, rows_t * r + per * c + i, half_t)
        as1[i, at, :] = (x1[i, at, :].astype(F32) + keep * update).astype(BF16)

        def send(o, inner):
            to = h * (key_n // 2) + lax.rem(c + o, key_n // 2)

            @pl.when(to != c)
            def _():
                a2_copy(i, 1, to, c).start()

            return inner

        lax.fori_loop(0, key_n // 2, send, 0)

    def between_one():
        moves.finish(1)
        widen_one(1)

    def sent_a2(o, carry):
        a2_copy(0, per, lax.rem(c + o, key_n), c).wait_send()
        return carry

    def wait_a2(o, carry):
        frm = lax.rem(c + key_n - o, key_n)
        copy = remote(
            as1.at[pl.ds(0, per), col_slice(c)], t2.at[pl.ds(frm * per, per)], a2_send.at[frm], a2_recv.at[frm], (r, frm)
        )
        copy.wait_recv()
        return carry

    moves_two = Gather(bias_b, gb_send, gb_recv, "zyx")
    halves = rows_t // KEYS

    def b2_row(a, o, to):
        return remote(sb.at[to * per + a], x2.at[a, row_slice(r)], b2_send.at[o], b2_recv.at[a], (to, c))

    def b2_own(a):
        return pltpu.make_async_copy(sb.at[r * per + a], x2.at[a, row_slice(r)], b2_recv.at[a])

    def send_b2(a, carry):
        def send(o, inner):
            b2_row(a, o, lax.rem(r + o, row_n)).start()
            return inner

        lax.fori_loop(1, row_n, send, 0)
        b2_own(a).start()
        return carry

    def wait_b2(a):
        pltpu.make_async_copy(x2.at[a], x2.at[a], b2_recv.at[a]).wait()

    def sent_b2(o, carry):
        to = lax.rem(r + o, row_n)
        rows_out = sb.at[pl.ds(to * per, per)]
        remote(rows_out, rows_out, b2_send.at[o], b2_recv.at[0], (to, c)).wait_send()
        return carry

    def second_whole():
        lax.fori_loop(1, key_n, wait_a2, 0)
        t2[pl.ds(per * c, per)] = as1[:, col_slice(c)]

    def second_bias():
        tile_f[...] = layer_norm(t2[...].astype(F32), gain_ref[1:2], shift_ref[1:2])
        acc = jnp.zeros((rows_t, LANES), F32)
        for k in range(0, KEYS, 2):
            left = jnp.concatenate(
                [jnp.concatenate([tile_f[h * KEYS + kk] for h in range(halves)], axis=0) for kk in (k, k + 1)], axis=1
            ).astype(BF16)
            right = jnp.concatenate([pick(1, k), pick(1, k + 1)], axis=0)
            acc = acc + jnp.dot(left, right, preferred_element_type=F32)
        bias_b[y, core, z, xx] = acc.astype(BF16)
        moves_two.start_one()

    early = z < z_n // 2
    late = jnp.logical_not(early)

    def early_bias():
        @pl.when(early)
        def _():
            second_whole()
            second_bias()

    attend(0, unit_one, {per - 3: lambda: moves.pass_on(1), per - 2: between_one, 2 * per - 2: early_bias})
    moves_two.start_three(0)
    @pl.when(late)
    def _():
        second_whole()
        second_bias()

    tile_f[...] = t2[...].astype(F32)
    for j in range(cols_t):
        sb[j] = tile_f[:, j, :].astype(BF16)
    lax.fori_loop(0, per, send_b2, 0)
    moves_two.pass_on(0)
    moves.drain()
    lax.fori_loop(1, key_n, sent_a2, 0)

    def late_row(a, carry):
        wait_b2(a)
        prepare(1, x2, a)
        return carry

    lax.fori_loop(0, 1, late_row, 0)
    moves_two.start_three(1)
    lax.fori_loop(1, per, late_row, 0)
    moves_two.finish(0)

    def widen_two(h):
        def widen(g, carry):
            for gg in range(row_n * halves):
                rr, hh = gg // halves, gg % halves
                block = bias_b[rr // 2, rr % 2, g // x_n, lax.rem(g, x_n), hh * KEYS : (hh + 1) * KEYS, :].astype(F32)
                bias_s[col_slice(g), gg * LANES : (gg + 1) * LANES] = block + key_bias(gg)
            return carry

        lax.fori_loop(h * key_n // 2, (h + 1) * key_n // 2, widen, 0)

    widen_two(0)

    def c2_copy(i, n, to, frm):
        return remote(
            np2.at[pl.ds(i, n), row_slice(to)], fin.at[pl.ds(frm * per + i, n)], c2_send.at[to], c2_recv.at[frm], (to, c)
        )

    def unit_two(i, h, at, update):
        keep = kept(h * half_t, cols_t * c + per * r + i, half_t)
        update = (keep * update).astype(BF16).astype(F32)
        np2[i, at, :] = (x2[i, at, :].astype(F32) + update).astype(BF16)

        def send(o, inner):
            to = h * (row_n // 2) + lax.rem(r + o, row_n // 2)

            @pl.when(to != r)
            def _():
                c2_copy(i, 1, to, r).start()

            return inner

        lax.fori_loop(0, row_n // 2, send, 0)

    def between_two():
        moves_two.finish(1)
        widen_two(1)

    attend(1, unit_two, {per - 3: lambda: moves_two.pass_on(1), per - 2: between_two})
    fin[pl.ds(per * r, per)] = np2[:, row_slice(r)]
    moves_two.drain()
    lax.fori_loop(1, row_n, sent_b2, 0)

    def wait_c2(o, carry):
        c2_copy(0, per, lax.rem(r + o, row_n), r).wait_send()
        frm = lax.rem(r + row_n - o, row_n)
        copy = remote(
            np2.at[pl.ds(0, per), row_slice(r)], fin.at[pl.ds(frm * per, per)], c2_send.at[frm], c2_recv.at[frm], (frm, c)
        )
        copy.wait_recv()
        return carry

    lax.fori_loop(1, row_n, wait_c2, 0)


def local(row_n, key_n, pair_rep, token_mask, norm_gain, norm_shift, w_proj, w_bias, gate_bias, w_out):
    rows_t, cols_t, channels = pair_rep.shape
    tokens = token_mask.shape[0]
    per = tokens // (row_n * key_n)
    groups = tokens // KEYS
    width = groups * LANES
    y_n, z_n = row_n // 2, int(round(key_n**0.5))
    slots = y_n - 1 + 2 * y_n * (z_n - 1) + y_n * z_n
    vmem, dma = pltpu.VMEM, pltpu.SemaphoreType.DMA
    buf = (y_n, 2, z_n, z_n, rows_t, LANES)
    turned = pl.pallas_call(
        functools.partial(kernel, tokens, row_n, key_n),
        out_shape=jax.ShapeDtypeStruct((cols_t, rows_t, channels), BF16),
        in_specs=[pl.BlockSpec(memory_space=pl.ANY if i in (0, 4, 7) else pltpu.VMEM) for i in range(8)],
        out_specs=pl.BlockSpec(memory_space=pltpu.VMEM),
        scratch_shapes=[
            vmem((per, tokens, LANES), BF16),
            vmem((per, tokens, LANES), BF16),
            vmem((per, tokens, LANES), BF16),
            vmem((per, tokens, LANES), BF16),
            vmem((rows_t, cols_t, LANES), BF16),
            vmem((cols_t, rows_t, LANES), BF16),
            vmem((rows_t, cols_t, LANES), F32),
            vmem(buf, BF16),
            vmem(buf, BF16),
            vmem((tokens, width), F32),
            vmem((per, tokens, LANES), BF16),
            vmem((per, width, LANES), BF16),
            vmem((per, width, 2 * LANES), BF16),
            vmem((per, tokens, LANES), F32),
            vmem((tokens // 2, width), F32),
            vmem((tokens // 2, width), F32),
            vmem((tokens // 2, width), BF16),
            vmem((tokens // 2, width), BF16),
            vmem((2, tokens // 2, LANES), F32),
            vmem((2, LANES, LANES), BF16),
            vmem((rows_t, cols_t, LANES), BF16),
            vmem(w_proj.shape, BF16),
            vmem(w_out.shape, BF16),
            dma((3,)),
            dma((key_n,)), dma((key_n,)), dma((key_n,)), dma((key_n,)),
            dma((row_n,)), dma((row_n,)), dma((row_n,)), dma((row_n,)),
            dma((slots,)), dma((slots,)), dma((slots,)), dma((slots,)),
        ],
        compiler_params=pltpu.CompilerParams(
            collective_id=0, has_side_effects=True, vmem_limit_bytes=56 * 2**20
        ),
        name="triangle_attention",
    )(
        pair_rep, token_mask.reshape(-1, min(tokens, LANES)), norm_gain, norm_shift, w_proj, w_bias.transpose(0, 2, 1), gate_bias,
        w_out,
    )
    return turned.transpose(1, 0, 2)


def solution(mesh):
    row_n, key_n = mesh.shape["rows"], mesh.shape["keys"]
    in_specs = (P("rows", "keys", None), P(), P(), P(), P(), P(), P(), P())
    out_specs = P("rows", "keys", None)
    return jax.shard_map(
        functools.partial(local, row_n, key_n), mesh=mesh, in_specs=in_specs, out_specs=out_specs, check_vma=False
    )
```

```python
import functools

import jax
import jax.numpy as jnp
from jax import lax
from jax.experimental import pallas as pl
from jax.experimental.pallas import tpu as pltpu
from jax.sharding import PartitionSpec as P

MESH = pl.DeviceIdType.MESH
LOG2E = 1.4426950408889634
F32 = jnp.float32
BF16 = jnp.bfloat16
KEYS = 32
HEADS = 4
HEAD = 32
LANES = 128
CHUNK = 256


def layer_norm(values, gain, shift):
    center = jnp.mean(values, axis=-1, keepdims=True)
    moved = values - center
    spread = jnp.mean(moved * moved, axis=-1, keepdims=True)
    return moved * lax.rsqrt(spread + 1e-05) * gain + shift


def head_max(m, lane):
    out = None
    for h in range(HEADS):
        mine = lane // KEYS == h
        largest = jnp.max(jnp.where(mine, m, -jnp.inf), axis=-1, keepdims=True)
        out = largest if out is None else jnp.where(mine, largest, out)
    return jnp.broadcast_to(out, m.shape)


def kernel(
    tokens, row_n, key_n,
    x_hbm, mask_ref, gain_ref, shift_ref, wp_hbm, wb_ref, gb_ref, wo_hbm,
    fin,
    x1, x2, as1, np2, t2, sb, tile_f, bias_a, bias_b, bias_s, q_s, k_s, v_s, g_s,
    s_even, s_odd, p_even, p_odd, top_s, wr_s, x_ref, wp_ref, wo_ref, x_sem,
    a1_send, a1_recv, a2_send, a2_recv, b2_send, b2_recv, c2_send, c2_recv,
    ga_send, ga_recv, gb_send, gb_recv,
):
    rows_t, cols_t = tokens // row_n, tokens // key_n
    per = tokens // (row_n * key_n)
    groups = tokens // KEYS
    y_n = row_n // 2
    z_n = x_n = int(round(key_n**0.5))
    half_t = tokens // 2
    r, c = lax.axis_index("rows"), lax.axis_index("keys")
    y, core = r // 2, r % 2
    z, xx = c // x_n, c % x_n
    lane = lax.broadcasted_iota(jnp.int32, (1, LANES), 1)

    barrier = pltpu.get_barrier_semaphore()
    piece = rows_t // 4
    x_copies = [
        pltpu.make_async_copy(
            x_hbm.at[i * piece : (i + 1) * piece], x_ref.at[i * piece : (i + 1) * piece], x_sem.at[2 + i]
        )
        for i in range(4)
    ]
    for copy in x_copies:
        copy.start()
    w_copies = (
        pltpu.make_async_copy(wp_hbm, wp_ref, x_sem.at[0]),
        pltpu.make_async_copy(wo_hbm, wo_ref, x_sem.at[1]),
    )
    for copy in w_copies:
        copy.start()

    def greet_keys(o, carry):
        pl.semaphore_signal(barrier, inc=1, device_id=(r, lax.rem(c + o, key_n)), device_id_type=MESH)
        return carry

    def greet_rows(o, carry):
        pl.semaphore_signal(barrier, inc=1, device_id=(lax.rem(r + o, row_n), c), device_id_type=MESH)
        return carry

    lax.fori_loop(1, key_n, greet_keys, 0)
    lax.fori_loop(1, row_n, greet_rows, 0)

    def greet_planes(o, carry):
        far = lax.rem(y + 1 + o // (z_n - 1), y_n) * 2 + core
        step = 1 + o % (z_n - 1)
        pl.semaphore_signal(
            barrier, inc=1, device_id=(far, lax.rem(z + step, z_n) * x_n + xx), device_id_type=MESH
        )
        pl.semaphore_signal(
            barrier, inc=1, device_id=(far, z * x_n + lax.rem(xx + step, x_n)), device_id_type=MESH
        )
        return carry

    planes = (y_n - 1) * (z_n - 1)
    lax.fori_loop(0, planes, greet_planes, 0)

    real = jnp.sum(mask_ref[...], keepdims=True)

    def key_bias(g):
        key = g * KEYS + lane % KEYS
        return jnp.where(key < real, 0.0, -1000000000.0)

    def kept(first, token, count):
        at = first + lax.broadcasted_iota(jnp.int32, (count, LANES), 0)
        return jnp.where(jnp.logical_and(at < real, token < real), 1.0, 0.0)

    lane_k = lax.broadcasted_iota(jnp.int32, (LANES, LANES), 1)
    sub_k = lax.broadcasted_iota(jnp.int32, (LANES, LANES), 0)
    ones = jnp.where(lane_k // HEAD == sub_k // KEYS, 1.0, 0.0).astype(BF16)

    def put_ones(i, carry):
        for g in range(groups):
            v_s[i, g * LANES : (g + 1) * LANES, LANES:] = ones
        return carry

    spread = lax.broadcasted_iota(jnp.int32, (HEADS, LANES), 0) == lax.broadcasted_iota(jnp.int32, (HEADS, LANES), 1) // KEYS
    spread = jnp.where(spread, 1.0, 0.0).astype(BF16)
    for m in range(2):
        wr_s[m] = lax.dot_general(
            wb_ref[m], spread, (((0,), (0,)), ((), ())), preferred_element_type=F32
        ).astype(BF16)

    def remote(src, dst, send, recv, device):
        return pltpu.make_async_remote_copy(
            src_ref=src, dst_ref=dst, send_sem=send, recv_sem=recv,
            device_id=device, device_id_type=MESH,
        )

    def col_slice(which):
        return pl.ds(pl.multiple_of(which * cols_t, cols_t), cols_t)

    def row_slice(which):
        return pl.ds(pl.multiple_of(which * rows_t, rows_t), rows_t)

    def send_a1(o, carry):
        to = lax.rem(c + o, key_n)
        remote(x_ref.at[pl.ds(to * per, per)], x1.at[:, col_slice(c)], a1_send.at[o], a1_recv.at[o], (r, to)).start()
        return carry

    def wait_a1(o, carry):
        to = lax.rem(c + key_n - o, key_n)
        copy = remote(x_ref.at[pl.ds(to * per, per)], x1.at[:, col_slice(to)], a1_send.at[o], a1_recv.at[o], (r, to))
        copy.wait_send()
        copy.wait_recv()
        return carry

    size = {"y": y_n, "z": z_n, "x": x_n}
    place = {"y": y, "z": z, "x": xx}

    def device(which_core, **at):
        at = {**place, **at}
        return (at["y"] * 2 + which_core, at["z"] * x_n + at["x"])

    def shifted(axis, d):
        return lax.rem(place[axis] + d, size[axis])

    class Gather:
        def __init__(self, buf, send, recv, axes):
            self.buf, self.send, self.recv = buf, send, recv
            self.first, self.others = axes[0], axes[1:]
            self.parts = size[axes[0]]
            self.turns = size[axes[1]] - 1

        def block(self, which_core, **at):
            at = {**place, **at}
            return self.buf.at[at["y"], which_core, at["z"], at["x"]]

        def copy(self, slot, ref, to):
            return remote(ref, ref, self.send.at[slot], self.recv.at[slot], to)

        def line(self, p, which_core, **at):
            u, v = self.others if p % 2 == 0 else self.others[::-1]
            return self.block(which_core, **{self.first: p, u: slice(None), v: at.get("v", place[v])})

        def one(self, o):
            first, (a, b) = self.first, self.others
            odd = place[first] % 2
            n = self.turns + 1
            at = {
                first: lax.rem(place[first] + o // n, self.parts),
                a: lax.rem(place[a] + (o % n) * (1 - odd), size[a]),
                b: lax.rem(place[b] + (o % n) * odd, size[b]),
            }
            return self.copy(o - 1, self.block(core), device(core, **at))

        def wait_one(self, p):
            u = self.others[p % 2]
            away = lax.rem(place[self.first] + self.parts - p, self.parts)
            for d in range(self.turns + 1):
                at = {self.first: p, u: shifted(u, size[u] - d)}
                arrived = self.copy(away * (self.turns + 1) + d - 1, self.block(core, **at), device(core, **at))
                if d:
                    arrived.wait_recv()
                else:
                    pl.when(away != 0)(arrived.wait_recv)

        def three(self, p, d, out):
            v = self.others[1 - p % 2]
            slot = self.parts * (self.turns + 1) - 1 + p * self.turns + d - 1
            near = shifted(v, size[v] - d)
            if out:
                return self.copy(slot, self.line(p, core), device(core, **{v: shifted(v, d)}))
            return self.copy(slot, self.line(p, core, v=near), device(core, **{v: near}))

        def mate(self, p, d, out):
            v = self.others[1 - p % 2]
            slot = self.parts * (self.turns + 1) - 1 + self.parts * self.turns + p * (self.turns + 1) + d
            near = shifted(v, size[v] - d)
            return self.copy(slot, self.line(p, core if out else 1 - core, v=near), device(1 - core))

        def steps(self):
            return sorted(range(1, self.turns + 1), key=lambda d: min(d, self.turns + 1 - d))

        def start_one(self):
            def send(o, carry):
                self.one(o).start()
                return carry

            lax.fori_loop(1, self.parts * (self.turns + 1), send, 0)

        def half(self, h):
            return range(h * self.parts // 2, (h + 1) * self.parts // 2)

        def start_three(self, h):
            for p in self.half(h):
                self.wait_one(p)
                for d in self.steps():
                    self.three(p, d, True).start()
                self.mate(p, 0, True).start()

        def pass_on(self, h):
            for d in self.steps():
                for p in self.half(h):
                    self.three(p, d, False).wait_recv()
                    self.mate(p, d, True).start()

        def finish(self, h):
            for p in self.half(h):
                for d in range(self.turns + 1):
                    self.mate(p, d, False).wait_recv()

        def drain(self):
            def sent(o, carry):
                self.one(o).wait_send()
                return carry

            lax.fori_loop(1, self.parts * (self.turns + 1), sent, 0)
            for p in range(self.parts):
                for d in self.steps():
                    self.three(p, d, True).wait_send()
                for d in range(self.turns + 1):
                    self.mate(p, d, True).wait_send()

    lane_q = lax.broadcasted_iota(jnp.int32, (KEYS, LANES), 1)

    def prepare(m, xs, i):
        normed = layer_norm(xs[i].astype(F32), gain_ref[m : m + 1], shift_ref[m : m + 1]).astype(BF16)

        def project(part):
            return jnp.dot(normed, wp_ref[m, :, part * LANES : (part + 1) * LANES], preferred_element_type=F32)

        q_s[i] = (project(0) * HEAD**-0.5).astype(BF16)
        k = project(1).astype(BF16)
        v = project(2).astype(BF16)
        g_s[i] = jax.nn.sigmoid(project(3) + gb_ref[m : m + 1])
        for g in range(groups):
            kg = k[g * KEYS : (g + 1) * KEYS]
            vg = v[g * KEYS : (g + 1) * KEYS]
            for h in range(HEADS):
                mine = lane_q // HEAD == h
                at = g * LANES + h * KEYS
                k_s[i, at : at + KEYS, :] = jnp.where(mine, kg, jnp.zeros_like(kg))
                v_s[i, at : at + KEYS, :LANES] = jnp.where(mine, vg, jnp.zeros_like(vg))

    width = groups * LANES

    def score_chunk(row, at, s_s, n, top):
        s = lax.dot_general(
            q_s[row, at, :], k_s[row, n : n + CHUNK, :], (((1,), (1,)), ((), ())), preferred_element_type=F32
        )
        s = s + bias_s[at, n : n + CHUNK]
        s_s[:, n : n + CHUNK] = s
        for t in range(0, CHUNK, LANES):
            part = s[:, t : t + LANES]
            top = part if top is None else jnp.maximum(top, part)
        return top

    def weight_chunk(s_s, p_s, n, top):
        p_s[:, n : n + CHUNK] = jnp.exp2((s_s[:, n : n + CHUNK] - top) * LOG2E).astype(BF16)

    def attend(m, unit_done, hooks):
        units = 2 * per

        def where(unit):
            return lax.rem(unit, per), pl.ds(pl.multiple_of(unit // per * half_t, half_t), half_t)

        def scores(unit, s_s, slot, before=None):
            row, at = where(unit)
            top = None
            if before is not None:
                s_b, p_b, slot_b = before
                top_b = jnp.concatenate([top_s[slot_b]] * (CHUNK // LANES), axis=1)
            for n in range(0, width, CHUNK):
                if before is not None:
                    weight_chunk(s_b, p_b, n, top_b)
                top = score_chunk(row, at, s_s, n, top)
            top_s[slot] = head_max(top, lane)

        def weights(s_s, p_s, slot):
            top = jnp.concatenate([top_s[slot]] * (CHUNK // LANES), axis=1)
            for n in range(0, width, CHUNK):
                weight_chunk(s_s, p_s, n, top)

        def values(unit, p_s):
            row, at = where(unit)
            total = jnp.dot(p_s[...], v_s[row], preferred_element_type=F32)
            gated = (total[:, :LANES] / total[:, LANES:] * g_s[row, at, :]).astype(BF16)
            update = jnp.dot(gated, wo_ref[m], preferred_element_type=F32)
            unit_done(row, unit // per, at, update)

        scores(0, s_even, 0)

        def pair(t, carry):
            unit = 2 * t

            def run_hooks(odd):
                for after, hook in hooks.items():
                    if after % 2 == odd:
                        pl.when(t == after // 2)(hook)

            scores(unit + 1, s_odd, 1, (s_even, p_even, 0))
            values(unit, p_even)
            run_hooks(0)

            @pl.when(t < per - 1)
            def _():
                scores(unit + 2, s_even, 0, (s_odd, p_odd, 1))
                values(unit + 1, p_odd)

            @pl.when(t == per - 1)
            def _():
                weights(s_odd, p_odd, 1)
                values(unit + 1, p_odd)

            run_hooks(1)
            return carry

        lax.fori_loop(0, per, pair, 0)

    for i, copy in enumerate(x_copies):
        copy.wait()
        rows = slice(i * piece, (i + 1) * piece)
        tile_f[rows] = layer_norm(x_ref[rows].astype(F32), gain_ref[0:1], shift_ref[0:1])

    def pick(m, k):
        return jnp.where(lane_k % KEYS == k, wr_s[m], jnp.zeros((LANES, LANES), BF16))

    acc = jnp.zeros((rows_t, LANES), F32)
    for k in range(0, cols_t, 2):
        left = jnp.concatenate([tile_f[:, k, :], tile_f[:, k + 1, :]], axis=1).astype(BF16)
        right = jnp.concatenate([pick(0, k), pick(0, k + 1)], axis=0)
        acc = acc + jnp.dot(left, right, preferred_element_type=F32)
    bias_a[y, core, z, xx] = acc.astype(BF16)
    pl.semaphore_wait(barrier, key_n - 1 + row_n - 1 + 2 * planes)

    def more(m, xs, lo, hi):
        def one(i, carry):
            prepare(m, xs, i)
            return carry

        lax.fori_loop(lo, hi, one, 0)

    def widen_one(h):
        def widen(g, carry):
            at = pl.ds(pl.multiple_of(g * LANES, LANES), LANES)
            masked = key_bias(g)
            for rr in range(h * row_n // 2, (h + 1) * row_n // 2):
                block = bias_a[rr // 2, rr % 2, g // x_n, lax.rem(g, x_n)].astype(F32)
                bias_s[rr * rows_t : (rr + 1) * rows_t, at] = block + masked
            return carry

        lax.fori_loop(0, key_n, widen, 0)

    moves = Gather(bias_a, ga_send, ga_recv, "yzx")
    moves.start_one()
    lax.fori_loop(1, key_n, send_a1, 0)
    x1[:, col_slice(c)] = x_ref[pl.ds(c * per, per)]
    lax.fori_loop(0, per, put_ones, 0)
    for copy in w_copies:
        copy.wait()
    moves.start_three(0)
    lax.fori_loop(1, key_n, wait_a1, 0)
    more(0, x1, 0, 1)
    moves.start_three(1)
    more(0, x1, 1, per)
    moves.pass_on(0)
    moves.finish(0)
    widen_one(0)

    def a2_copy(i, n, to, frm):
        return remote(
            as1.at[pl.ds(i, n), col_slice(to)], t2.at[pl.ds(frm * per + i, n)], a2_send.at[to], a2_recv.at[frm], (r, to)
        )

    def unit_one(i, h, at, update):
        keep = kept(h * half_t, rows_t * r + per * c + i, half_t)
        as1[i, at, :] = (x1[i, at, :].astype(F32) + keep * update).astype(BF16)

        def send(o, inner):
            to = h * (key_n // 2) + lax.rem(c + o, key_n // 2)

            @pl.when(to != c)
            def _():
                a2_copy(i, 1, to, c).start()

            return inner

        lax.fori_loop(0, key_n // 2, send, 0)

    def between_one():
        moves.finish(1)
        widen_one(1)

    def sent_a2(o, carry):
        a2_copy(0, per, lax.rem(c + o, key_n), c).wait_send()
        return carry

    def wait_a2(o, carry):
        frm = lax.rem(c + key_n - o, key_n)
        copy = remote(
            as1.at[pl.ds(0, per), col_slice(c)], t2.at[pl.ds(frm * per, per)], a2_send.at[frm], a2_recv.at[frm], (r, frm)
        )
        copy.wait_recv()
        return carry

    moves_two = Gather(bias_b, gb_send, gb_recv, "zyx")
    halves = rows_t // KEYS

    def b2_row(a, o, to):
        return remote(sb.at[to * per + a], x2.at[a, row_slice(r)], b2_send.at[o], b2_recv.at[a], (to, c))

    def b2_own(a):
        return pltpu.make_async_copy(sb.at[r * per + a], x2.at[a, row_slice(r)], b2_recv.at[a])

    def send_b2(a, carry):
        def send(o, inner):
            b2_row(a, o, lax.rem(r + o, row_n)).start()
            return inner

        lax.fori_loop(1, row_n, send, 0)
        b2_own(a).start()
        return carry

    def wait_b2(a):
        pltpu.make_async_copy(x2.at[a], x2.at[a], b2_recv.at[a]).wait()

    def sent_b2(o, carry):
        to = lax.rem(r + o, row_n)
        rows_out = sb.at[pl.ds(to * per, per)]
        remote(rows_out, rows_out, b2_send.at[o], b2_recv.at[0], (to, c)).wait_send()
        return carry

    def second_whole():
        lax.fori_loop(1, key_n, wait_a2, 0)
        t2[pl.ds(per * c, per)] = as1[:, col_slice(c)]

    def second_bias():
        tile_f[...] = layer_norm(t2[...].astype(F32), gain_ref[1:2], shift_ref[1:2])
        acc = jnp.zeros((rows_t, LANES), F32)
        for k in range(0, KEYS, 2):
            left = jnp.concatenate(
                [jnp.concatenate([tile_f[h * KEYS + kk] for h in range(halves)], axis=0) for kk in (k, k + 1)], axis=1
            ).astype(BF16)
            right = jnp.concatenate([pick(1, k), pick(1, k + 1)], axis=0)
            acc = acc + jnp.dot(left, right, preferred_element_type=F32)
        bias_b[y, core, z, xx] = acc.astype(BF16)
        moves_two.start_one()

    early = z < z_n // 2
    late = jnp.logical_not(early)

    def early_bias():
        @pl.when(early)
        def _():
            second_whole()
            second_bias()

    attend(0, unit_one, {per - 3: lambda: moves.pass_on(1), per - 2: between_one, 2 * per - 2: early_bias})
    moves_two.start_three(0)
    @pl.when(late)
    def _():
        second_whole()
        second_bias()

    tile_f[...] = t2[...].astype(F32)
    for j in range(cols_t):
        sb[j] = tile_f[:, j, :].astype(BF16)
    lax.fori_loop(0, per, send_b2, 0)
    moves_two.pass_on(0)
    moves.drain()
    lax.fori_loop(1, key_n, sent_a2, 0)

    def late_row(a, carry):
        wait_b2(a)
        prepare(1, x2, a)
        return carry

    lax.fori_loop(0, 1, late_row, 0)
    moves_two.start_three(1)
    lax.fori_loop(1, per, late_row, 0)
    moves_two.finish(0)

    def widen_two(h):
        def widen(g, carry):
            for gg in range(row_n * halves):
                rr, hh = gg // halves, gg % halves
                block = bias_b[rr // 2, rr % 2, g // x_n, lax.rem(g, x_n), hh * KEYS : (hh + 1) * KEYS, :].astype(F32)
                bias_s[col_slice(g), gg * LANES : (gg + 1) * LANES] = block + key_bias(gg)
            return carry

        lax.fori_loop(h * key_n // 2, (h + 1) * key_n // 2, widen, 0)

    widen_two(0)

    def c2_copy(i, n, to, frm):
        return remote(
            np2.at[pl.ds(i, n), row_slice(to)], fin.at[pl.ds(frm * per + i, n)], c2_send.at[to], c2_recv.at[frm], (to, c)
        )

    def unit_two(i, h, at, update):
        keep = kept(h * half_t, cols_t * c + per * r + i, half_t)
        update = (keep * update).astype(BF16).astype(F32)
        np2[i, at, :] = (x2[i, at, :].astype(F32) + update).astype(BF16)

        def send(o, inner):
            to = h * (row_n // 2) + lax.rem(r + o, row_n // 2)

            @pl.when(to != r)
            def _():
                c2_copy(i, 1, to, r).start()

            return inner

        lax.fori_loop(0, row_n // 2, send, 0)

    def between_two():
        moves_two.finish(1)
        widen_two(1)

    attend(1, unit_two, {per - 3: lambda: moves_two.pass_on(1), per - 2: between_two})
    fin[pl.ds(per * r, per)] = np2[:, row_slice(r)]
    moves_two.drain()
    lax.fori_loop(1, row_n, sent_b2, 0)

    def wait_c2(o, carry):
        c2_copy(0, per, lax.rem(r + o, row_n), r).wait_send()
        frm = lax.rem(r + row_n - o, row_n)
        copy = remote(
            np2.at[pl.ds(0, per), row_slice(r)], fin.at[pl.ds(frm * per, per)], c2_send.at[frm], c2_recv.at[frm], (frm, c)
        )
        copy.wait_recv()
        return carry

    lax.fori_loop(1, row_n, wait_c2, 0)


def local(row_n, key_n, pair_rep, token_mask, norm_gain, norm_shift, w_proj, w_bias, gate_bias, w_out):
    rows_t, cols_t, channels = pair_rep.shape
    tokens = token_mask.shape[0]
    per = tokens // (row_n * key_n)
    groups = tokens // KEYS
    width = groups * LANES
    y_n, z_n = row_n // 2, int(round(key_n**0.5))
    slots = y_n - 1 + 2 * y_n * (z_n - 1) + y_n * z_n
    vmem, dma = pltpu.VMEM, pltpu.SemaphoreType.DMA
    buf = (y_n, 2, z_n, z_n, rows_t, LANES)
    turned = pl.pallas_call(
        functools.partial(kernel, tokens, row_n, key_n),
        out_shape=jax.ShapeDtypeStruct((cols_t, rows_t, channels), BF16),
        in_specs=[pl.BlockSpec(memory_space=pl.ANY if i in (0, 4, 7) else pltpu.VMEM) for i in range(8)],
        out_specs=pl.BlockSpec(memory_space=pltpu.VMEM),
        scratch_shapes=[
            vmem((per, tokens, LANES), BF16),
            vmem((per, tokens, LANES), BF16),
            vmem((per, tokens, LANES), BF16),
            vmem((per, tokens, LANES), BF16),
            vmem((rows_t, cols_t, LANES), BF16),
            vmem((cols_t, rows_t, LANES), BF16),
            vmem((rows_t, cols_t, LANES), F32),
            vmem(buf, BF16),
            vmem(buf, BF16),
            vmem((tokens, width), F32),
            vmem((per, tokens, LANES), BF16),
            vmem((per, width, LANES), BF16),
            vmem((per, width, 2 * LANES), BF16),
            vmem((per, tokens, LANES), F32),
            vmem((tokens // 2, width), F32),
            vmem((tokens // 2, width), F32),
            vmem((tokens // 2, width), BF16),
            vmem((tokens // 2, width), BF16),
            vmem((2, tokens // 2, LANES), F32),
            vmem((2, LANES, LANES), BF16),
            vmem((rows_t, cols_t, LANES), BF16),
            vmem(w_proj.shape, BF16),
            vmem(w_out.shape, BF16),
            dma((6,)),
            dma((key_n,)), dma((key_n,)), dma((key_n,)), dma((key_n,)),
            dma((row_n,)), dma((row_n,)), dma((row_n,)), dma((row_n,)),
            dma((slots,)), dma((slots,)), dma((slots,)), dma((slots,)),
        ],
        compiler_params=pltpu.CompilerParams(
            collective_id=0, has_side_effects=True, vmem_limit_bytes=56 * 2**20
        ),
        name="triangle_attention",
    )(
        pair_rep, token_mask.reshape(-1, min(tokens, LANES)), norm_gain, norm_shift, w_proj, w_bias.transpose(0, 2, 1), gate_bias,
        w_out,
    )
    return turned.transpose(1, 0, 2)


def solution(mesh):
    row_n, key_n = mesh.shape["rows"], mesh.shape["keys"]
    in_specs = (P("rows", "keys", None), P(), P(), P(), P(), P(), P(), P())
    out_specs = P("rows", "keys", None)
    return jax.shard_map(
        functools.partial(local, row_n, key_n), mesh=mesh, in_specs=in_specs, out_specs=out_specs, check_vma=False
    )
```
